512 devices in a mesh: slab: 8 (over z_hi, core), work: 64 (over x, z_lo, y).
Axes of the slice: x: 4, y: 8, z: 8 (z_hi: 4, z_lo: 2; z = z_hi * 2 + z_lo), core: 2. Of those that a mesh axis runs over, the one named last changes fastest.
Arguments:
- particle_data: bfloat16 [8192, 40960], P(('slab', 'work')), may hold values from -21 to 21
- optics_label: int32 [8192], P(('slab', 'work')), may hold values from 0 to 7
- half_set: int32 [8192], P(('slab', 'work')), may hold values from 0 to 1
- shift_offset: int32 [8192, 2], P(('slab', 'work')), may hold values from -4 to 4
- ctf_bank: float32 [8, 20480], replicated, may hold values from -1 to 1
- noise_power: float32 [20480], replicated, may hold values from 2 to 20
- half_maps: bfloat16 [2, 256, 40960], P(None, 'slab', 'work'), may hold values from -6 to 6
- orient_index: int32 [8], replicated, may hold values from 0 to 4607
Outputs:
- log_total: float32 [8192], P(('slab', 'work'))
- volume_update: float32 [2, 256, 40960], P(None, 'slab', 'work')
The draws below stay inside these ranges and needn't reach their ends.
All inputs are finite; a program needn't handle non-finite values.
Results may differ from the reference program's by a relative error of at most 0.007.
The reference program's roundings to bfloat16 on the way (of `slices`, `prepared` and `weights`) count: a program that leaves them out, or rounds other values in their place, can miss the bound.
Values may be sent and summed in bfloat16 or wider, within the bound.
A program may use at most 64 MiB of HBM per device.

```python
import math
import jax
import jax.numpy as jnp
from jax import lax

ORDER = 256
PIX = 20480
GRID = 4608
GROUPS = 8
ORIENTS = 8
P_DEV = 16
PARTICLES = 8192


def draw_particle_data(key, part):
    key = jax.random.fold_in(key, 11)
    values = jnp.clip(jax.random.normal(key, (PARTICLES, 2 * PIX), jnp.float32), -6.0, 6.0)
    return values.astype(jnp.bfloat16)


def place_ends(array, rng, least, largest):
    longest = array.shape.index(max(array.shape))
    spots = []
    for shift in (0, 1):
        where = [jax.random.randint(jax.random.fold_in(rng, axis), (), 0, length) for axis, length in enumerate(array.shape)]
        where[longest] = (where[longest] + shift) % array.shape[longest]
        spots.append(tuple(where))
    return array.at[spots[0]].set(least).at[spots[1]].set(largest)


def level_of(rng, shape, split, smallest, top_value):
    factor_of = 1.0
    for dim, blocks in split:
        draws = jax.random.uniform(jax.random.fold_in(jax.random.fold_in(rng, 6), dim), (blocks,), jnp.float32, smallest / len(split), top_value / len(split))
        factor_of = factor_of * jnp.repeat(jnp.exp(draws), shape[dim] // blocks).reshape((-1,) + (1,) * (len(shape) - 1 - dim))
    return factor_of


def centred(stream_key, extent, deviation, bound, pieces=(), kind=jnp.bfloat16):
    result = jax.random.normal(stream_key, extent, jnp.float32) * deviation
    if len(pieces) > 0:
        result = level_of(stream_key, extent, pieces, -0.22, 0.18) * result
    return jnp.clip(result, min=-bound, max=bound).astype(kind)


def setup_inputs(seed: int = 0) -> dict:
    arg_keys = jax.random.split(jax.random.key(seed), 9)
    particle_data = draw_particle_data(jax.random.fold_in(arg_keys[8], 71), 0)
    optics_label = place_ends(jax.random.randint(arg_keys[1], (PARTICLES,), 0, GROUPS), jax.random.fold_in(arg_keys[1], 1), 0, GROUPS - 1).astype(jnp.int32)
    half_set = place_ends(jax.random.randint(arg_keys[2], (PARTICLES,), 0, 2), jax.random.fold_in(arg_keys[2], 1), 0, 1).astype(jnp.int32)
    shift_offset = place_ends(jax.random.randint(arg_keys[3], (PARTICLES, 2), -4, 5), jax.random.fold_in(arg_keys[3], 1), -4, 4).astype(jnp.int32)
    ctf_bank = jnp.clip(jax.random.uniform(arg_keys[4], (GROUPS, PIX), jnp.float32, -1.0, 1.0), -1.0, 1.0)
    noise_power = jnp.clip(jnp.exp(jax.random.uniform(arg_keys[5], (PIX,), jnp.float32, math.log(2.0), math.log(20.0))), 2.0, 20.0)
    half_maps = centred(arg_keys[6], (2, ORDER, 2 * PIX), 1.0, 6.0, ((1, 8), (2, 64)))
    orient_index = place_ends(jax.random.randint(arg_keys[7], (ORIENTS,), 0, GRID), jax.random.fold_in(arg_keys[7], 1), 0, GRID - 1).astype(jnp.int32)
    return dict(particle_data=particle_data, optics_label=optics_label, half_set=half_set, shift_offset=shift_offset, ctf_bank=ctf_bank, noise_power=noise_power, half_maps=half_maps, orient_index=orient_index)


def pixel_coords():
    pixel = lax.iota(jnp.int32, PIX)
    coord_u = (pixel // ORDER).astype(jnp.float32)
    coord_v = (pixel % ORDER - ORDER // 2).astype(jnp.float32)
    return coord_u, coord_v


def sines_of(indices):
    theta = math.pi * (indices.astype(jnp.float32) + 0.5) / GRID - 0.5 * math.pi
    return jnp.sin(theta)


def tent_weights(orient_sines, planes):
    coord_u, coord_v = pixel_coords()
    depth = ORDER // 2 + orient_sines[:, None] * coord_v[None, :]
    nearness = jnp.maximum(0.0, 1.0 - jnp.abs(planes[None, :, None] - depth[:, None, :]))
    return jnp.concatenate([nearness, nearness], axis=2)


def reference(particle_data, optics_label, half_set, shift_offset, ctf_bank, noise_power, half_maps, orient_index):
    coord_u, coord_v = pixel_coords()

    def prepare_block(item_pair):
        block_data, block_labels, block_shift = item_pair
        shift_x = block_shift[:, 0:1].astype(jnp.float32)
        shift_y = block_shift[:, 1:2].astype(jnp.float32)
        phase_angle = -2.0 * math.pi * (coord_u[None, :] * shift_x + coord_v[None, :] * shift_y) / ORDER
        cosine = jnp.cos(phase_angle)
        sine_part = jnp.sin(phase_angle)
        values = block_data.astype(jnp.float32)
        real_part = values[:, :PIX]
        imag_part = values[:, PIX:]
        factor = ctf_bank[block_labels] / noise_power[None, :]
        shifted_real = (real_part * cosine - imag_part * sine_part) * factor
        shifted_imag = (real_part * sine_part + imag_part * cosine) * factor
        return jnp.concatenate([shifted_real, shifted_imag], axis=1).astype(jnp.bfloat16)

    prepared = lax.map(prepare_block, (particle_data.reshape(-1, P_DEV, 2 * PIX),
                                       optics_label.reshape(-1, P_DEV),
                                       shift_offset.reshape(-1, P_DEV, 2))).reshape(-1, 2 * PIX)
    orient_sines = sines_of(orient_index)
    planes = lax.iota(jnp.int32, ORDER).astype(jnp.float32)
    volumes = half_maps.astype(jnp.float32)

    def project(block_sines):
        tent_table = tent_weights(block_sines, planes)
        return jnp.einsum('ozc,hzc->hoc', tent_table, volumes, precision=lax.Precision.HIGHEST)

    blocks = lax.map(project, orient_sines.reshape(-1, 1))
    slices = jnp.transpose(blocks, (1, 0, 2, 3)).reshape(2, -1, 2 * PIX).astype(jnp.bfloat16)
    ctf_square = ctf_bank * ctf_bank / noise_power[None, :]

    def half_logits(half_index):
        slice_rows = slices[half_index]
        cross_terms = jnp.dot(prepared, slice_rows.T, preferred_element_type=jnp.float32)
        slice_float = slice_rows.astype(jnp.float32)
        magnitude = slice_float[:, :PIX] ** 2 + slice_float[:, PIX:] ** 2
        power_table = jnp.dot(ctf_square, magnitude.T, precision=lax.Precision.HIGHEST)
        return cross_terms - 0.5 * power_table[optics_label]

    logits = jnp.where(half_set[:, None] == 0, half_logits(0), half_logits(1))
    highest = jnp.max(logits, axis=1, keepdims=True)
    summed = jnp.sum(jnp.exp(logits - highest), axis=1, keepdims=True)
    log_total = highest + jnp.log(summed)
    weights = jnp.exp(logits - log_total).astype(jnp.bfloat16)
    zero_weight = jnp.zeros_like(weights)
    first_half = jnp.where(half_set[:, None] == 0, weights, zero_weight)
    second_half = jnp.where(half_set[:, None] == 1, weights, zero_weight)
    sums = jnp.stack([jnp.dot(first_half.T, prepared, preferred_element_type=jnp.float32),
                      jnp.dot(second_half.T, prepared, preferred_element_type=jnp.float32)], axis=1)

    def insert(running, item_pair):
        block_sums, block_sines = item_pair
        tent_table = tent_weights(block_sines, planes)
        return running + jnp.einsum('ozc,ohc->hzc', tent_table, block_sums, precision=lax.Precision.HIGHEST), None

    start_volume = jnp.zeros((2, ORDER, 2 * PIX), jnp.float32)
    volume_update, unused = lax.scan(insert, start_volume, (sums.reshape(-1, 1, 2, 2 * PIX), orient_sines.reshape(-1, 1)))
    return log_total[:, 0], volume_update
```

```python
import math

import jax
import jax.numpy as jnp
from jax import lax
from jax.experimental import pallas as pl
from jax.experimental.pallas import tpu as pltpu
from jax.sharding import PartitionSpec as P

ORDER = 256
PIX = 20480
GRID = 4608
GROUPS = 8
ORIENTS = 8
NX, NY, NZ = 4, 8, 8
PLANES = 32
BLOCK = 640
CHUNK = NY * BLOCK
ROWS = 2 * ORIENTS
MINE = 16
PAIR = 2 * MINE
LANES = 128
TILES = BLOCK // LANES
MESH = pl.DeviceIdType.MESH
F32 = jnp.float32
BF16 = jnp.bfloat16


def device(x, y, z, core):
    return {
        "slab": lax.div(z, 2) * 2 + core,
        "work": (x * 2 + lax.rem(z, 2)) * NY + y,
    }


def turn_of(steps):
    k = lax.bitwise_and(steps, 255)
    quadrant = lax.shift_right_logical(k + 32, 6)
    r = (k - 64 * quadrant).astype(F32) * F32(2.0 * math.pi / ORDER)
    r2 = r * r
    s = r * (1.0 + r2 * (-1.0 / 6 + r2 * (1.0 / 120 + r2 * (-1.0 / 5040 + r2 * (1.0 / 362880)))))
    c = 1.0 + r2 * (-0.5 + r2 * (1.0 / 24 + r2 * (-1.0 / 720 + r2 * (1.0 / 40320 - r2 * (1.0 / 3628800)))))
    odd = lax.bitwise_and(quadrant, 1) == 1
    low = jnp.where(odd, s, c)
    high = jnp.where(odd, c, s)
    turned = lax.bitwise_and(quadrant, 3)
    cosine = jnp.where((turned == 1) | (turned == 2), -low, low)
    sine = jnp.where(turned >= 2, -high, high)
    return cosine, -sine


def kernel(
    orient, label, half, shift, maps, data, ctf, noise,
    log_out, volume_out,
    tent, part, swap, own_half, z_in, slices, raw, meta, ctf_v, noise_v, square, turn_u, turn_v,
    prep, pad, mass, logit, other_logit, weight, x_out, x_in, own, y_out, y_in, z_out, total_in, total,
    local_sem, core_send, core_recv, raw_send, raw_recv, zs, zr, ag_ys, ag_xs, ag_r, xs, xr, ys, yr, ts, tr,
):
    slab = lax.axis_index("slab")
    work = lax.axis_index("work")
    core = lax.rem(slab, 2)
    zh = lax.div(slab, 2)
    x = lax.div(work, 2 * NY)
    zl = lax.rem(lax.div(work, NY), 2)
    y = lax.rem(work, NY)
    z = 2 * zh + zl
    far = 1 - core
    partner = device(x, y, z, far)

    def remote(src, dst, send, recv, target):
        return pltpu.make_async_remote_copy(
            src_ref=src, dst_ref=dst, send_sem=send, recv_sem=recv, device_id=target, device_id_type=MESH
        )

    def arrived(dst, recv):
        remote(dst, dst, recv, recv, partner).wait_recv()

    def left(src, send):
        remote(src, src, send, send, partner).wait_send()

    barrier = pltpu.get_barrier_semaphore()
    friends = [partner]
    friends += [device(x, y, lax.rem(z + d, NZ), k) for d in range(1, NZ) for k in range(2)]
    friends += [device(x, lax.rem(y + d, NY), z, core) for d in range(1, NY)]
    friends += [device(lax.rem(x + d, NX), y, z, core) for d in range(1, NX)]
    for friend in friends:
        pl.semaphore_signal(barrier, inc=1, device_id=friend, device_id_type=MESH)

    def columns(q, k):
        return pl.ds(pl.multiple_of(q * (2 * CHUNK) + k * CHUNK, LANES), CHUNK)

    local = [
        pltpu.make_async_copy(data.at[:, columns(q, core)], raw.at[core, q], local_sem.at[q]) for q in range(4)
    ]
    for q in range(2):
        local.append(pltpu.make_async_copy(ctf.at[:, columns(q, core)], ctf_v.at[q], local_sem.at[4 + q]))
        local.append(pltpu.make_async_copy(noise.at[:, columns(q, core)], noise_v.at[q], local_sem.at[6 + q]))
    for copy in local:
        copy.start()

    row8 = lax.broadcasted_iota(jnp.int32, (ORIENTS, LANES), 0)
    lane8 = lax.broadcasted_iota(jnp.int32, (ORIENTS, LANES), 1)
    index = jnp.zeros((ORIENTS, LANES), jnp.int32)
    for o in range(ORIENTS):
        index = jnp.where(row8 == o, orient[o], index)
    sines = jnp.sin(math.pi * (index.astype(F32) + 0.5) / GRID - 0.5 * math.pi)
    plane = (slab * PLANES + lax.broadcasted_iota(jnp.int32, (PLANES, LANES), 0)).astype(F32)
    lane1 = lax.broadcasted_iota(jnp.int32, (1, LANES), 1)
    for t in range(TILES):
        tile = slice(t * LANES, (t + 1) * LANES)
        coord_v = (lane1 - LANES + LANES * lax.rem(work + t, 2)).astype(F32)
        values = [maps[h, :, tile].astype(F32) for h in range(2)]
        found = [[], []]
        for o in range(ORIENTS):
            depth = ORDER // 2 + sines[o : o + 1, :] * coord_v
            near = jnp.maximum(0.0, 1.0 - jnp.abs(plane - depth))
            tent[o, :, tile] = near
            for h in range(2):
                found[h].append(jnp.sum(near * values[h], axis=0, keepdims=True))
        for h in range(2):
            part[h, :, tile] = jnp.concatenate(found[h], axis=0)

    row16 = lax.broadcasted_iota(jnp.int32, (MINE, LANES), 0)
    about = [jnp.zeros((MINE, LANES), jnp.int32) for _ in range(3)]
    across = jnp.zeros((ORIENTS, LANES), jnp.int32)
    for i in range(MINE):
        here = row16 == i
        about[0] = jnp.where(here, label[i], about[0])
        about[1] = jnp.where(here, shift[i, 0], about[1])
        about[2] = jnp.where(here, shift[i, 1], about[2])
        there = lane8 == core * MINE + i
        across = jnp.where(there & (row8 == 0), label[i], across)
        across = jnp.where(there & (row8 == 1), half[i], across)
    for j in range(3):
        meta[core, j] = about[j]
    meta[core, 3, 0:8, :] = across
    meta[core, 3, 8:16, :] = across

    pl.semaphore_wait(barrier, len(friends))

    swap_copy = remote(part.at[far], swap, core_send.at[0], core_recv.at[0], partner)
    swap_copy.start()
    meta_copy = remote(meta.at[core], meta.at[core], core_send.at[1], core_recv.at[1], partner)
    meta_copy.start()
    raw_copies = [
        remote(data.at[:, columns(q, far)], raw.at[core, q], raw_send.at[q], raw_recv.at[q], partner)
        for q in range(4)
    ]
    for copy in raw_copies:
        copy.start()

    swap_copy.wait_recv()
    own_half[...] = part[core] + swap[...]
    z_copies = [
        remote(own_half, z_in.at[slab], zs.at[d], zr.at[slab], device(x, y, lax.rem(z + d, NZ), zl))
        for d in range(NZ)
    ]
    for copy in z_copies[1:]:
        copy.start()

    @pl.when(core == zl)
    def _():
        z_in[slab] = own_half[...]

    @pl.when(core != zl)
    def _():
        z_copies[0].start()

    for copy in local:
        copy.wait()
    arrived(meta.at[far], core_recv.at[1])
    for q in range(4):
        arrived(raw.at[far, q], raw_recv.at[q])

    label32 = jnp.concatenate([meta[0, 0], meta[1, 0]], axis=0)
    move_u = jnp.concatenate([meta[0, 1], meta[1, 1]], axis=0)
    move_v = jnp.concatenate([meta[0, 2], meta[1, 2]], axis=0)
    lane32 = lax.broadcasted_iota(jnp.int32, (PAIR, LANES), 1)
    for v in range(2):
        cosine, sine = turn_of((lane32 + (v - 1) * LANES) * move_v)
        turn_v[v, 0] = cosine
        turn_v[v, 1] = sine
    per_chunk = CHUNK // ORDER
    coord_u = lane32 + core * per_chunk + jnp.where(lane32 >= per_chunk, per_chunk, 0)
    cosine, sine = turn_of(coord_u * move_u)
    for t in range(2 * per_chunk):
        turn_u[t, 0] = jnp.broadcast_to(cosine[:, t : t + 1], (PAIR, LANES))
        turn_u[t, 1] = jnp.broadcast_to(sine[:, t : t + 1], (PAIR, LANES))
    bits = [lax.bitwise_and(label32, 1 << j) != 0 for j in range(3)]

    def prepare(step, carry):
        q = lax.div(step, 4)
        pair = lax.rem(step, 4)
        span = pl.ds(pl.multiple_of(pair * (2 * BLOCK), LANES), 2 * BLOCK)
        filters = ctf_v[q, :, span]
        variance = noise_v[q, :, span]
        scaled = filters / variance
        squared = filters * filters / variance
        pieces = [[raw[k, q + 2 * i, :, span] for k in range(2)] for i in range(2)]
        for t in range(2 * TILES):
            tile = slice(t * LANES, (t + 1) * LANES)
            block = pair * 2 + t // TILES
            inside = slice((t % TILES) * LANES, (t % TILES + 1) * LANES)
            square[q * NY + block, :, inside] = squared[:, tile]
            wide = [jnp.broadcast_to(scaled[g : g + 1, tile], (PAIR, LANES)) for g in range(GROUPS)]
            wide = [jnp.where(bits[0], wide[2 * j + 1], wide[2 * j]) for j in range(4)]
            wide = [jnp.where(bits[1], wide[2 * j + 1], wide[2 * j]) for j in range(2)]
            factor = jnp.where(bits[2], wide[1], wide[0])
            u = step * 5 + t // 2
            cos_u, sin_u, cos_v, sin_v = turn_u[u, 0], turn_u[u, 1], turn_v[t % 2, 0], turn_v[t % 2, 1]
            cos_q = cos_u * cos_v - sin_u * sin_v
            sin_q = sin_u * cos_v + cos_u * sin_v
            real, imag = [
                jnp.concatenate([pieces[i][0][:, tile], pieces[i][1][:, tile]], axis=0).astype(F32)
                for i in range(2)
            ]
            prep[q, block, :, inside] = ((real * cos_q - imag * sin_q) * factor).astype(BF16)
            prep[q + 2, block, :, inside] = ((real * sin_q + imag * cos_q) * factor).astype(BF16)
        return carry

    lax.fori_loop(0, 8, prepare, 0)

    for d in range(1, 8):
        s = lax.rem(slab + d, 8)
        arrived(z_in.at[s], zr.at[s])

    @pl.when(core != zl)
    def _():
        arrived(z_in.at[slab], zr.at[slab])

    halves = [z_in[h] + z_in[2 + h] + z_in[4 + h] + z_in[6 + h] for h in range(2)]
    slices[x * NY + y] = jnp.concatenate(halves, axis=0).astype(BF16)

    def block_copy(b, send, target):
        return remote(slices.at[b], slices.at[b], send, ag_r.at[b], target)

    turns = [0, 1, 7, 2, 6, 3, 5, 4]
    for d in (4, 3, 5, 2, 6, 1, 7):
        block_copy(x * NY + y, ag_ys.at[d], device(x, lax.rem(y + d, NY), z, core)).start()
    for d in turns:
        b = x * NY + lax.rem(y + d, NY)
        if d:
            arrived(slices.at[b], ag_r.at[b])
        for e in (2, 1, 3):
            block_copy(b, ag_xs.at[e - 1, d], device(lax.rem(x + e, NX), y, z, core)).start()

    def score(xx, wait):
        def step(j, carry):
            yy = lax.rem(y + lax.rem(lax.div(j + 1, 2) * (1 + 6 * lax.rem(j + 1, 2)), 8), NY)
            b = xx * NY + yy
            if wait:
                arrived(slices.at[b], ag_r.at[b])
            cross, sums = carry
            rows = slices[b]
            cross = cross + lax.dot_general(
                rows, prep[xx, yy], (((1,), (1,)), ((), ())), preferred_element_type=F32
            )
            wide = rows.astype(F32)
            pb = lax.rem(xx, 2) * NY + yy
            sums = list(sums)
            for t in range(TILES):
                tile = slice(t * LANES, (t + 1) * LANES)
                size = wide[:, tile] * wide[:, tile]
                gain = square[pb, :, tile]
                for g in range(GROUPS):
                    sums[g] = sums[g] + size * gain[g : g + 1, :]
            return cross, tuple(sums)

        return step

    carry = (jnp.zeros((ROWS, PAIR), F32), tuple(jnp.zeros((ROWS, LANES), F32) for _ in range(GROUPS)))
    for e in (0, 1, 3, 2):
        carry = lax.fori_loop(0, NY, score(lax.rem(x + e, NX), e > 0), carry)
    cross, sums = carry

    about_lanes = meta[0, 3] + meta[1, 3]
    label_lane = about_lanes[0:1, :]
    half_lane = about_lanes[1:2, :]
    pad[...] = jnp.zeros((ROWS, LANES), F32)
    pad[:, 0:PAIR] = cross
    value = pad[...]
    for g in range(GROUPS):
        power = jnp.sum(sums[g], axis=1, keepdims=True)
        value = value - jnp.where(label_lane == g, 0.5 * power, 0.0)
    logit[...] = jnp.where(half_lane == 0, value[0:8, :], value[8:16, :])
    logit_copy = remote(logit, other_logit, core_send.at[2], core_recv.at[2], partner)
    logit_copy.start()
    logit_copy.wait_recv()
    logits = logit[...] + other_logit[...]
    highest = jnp.max(logits, axis=0, keepdims=True)
    log_total = highest + jnp.log(jnp.sum(jnp.exp(logits - highest), axis=0, keepdims=True))
    weights = jnp.exp(logits - log_total)
    both = [jnp.where(half_lane == h, weights, 0.0) for h in range(2)]
    weight[...] = jnp.concatenate(both, axis=0).astype(BF16)
    log_out[...] = jnp.where(core == 0, log_total[:, 0:MINE], log_total[:, MINE:PAIR])

    shares = weight[:, 0:PAIR]

    def weighted(xx, yy):
        return jnp.dot(shares, prep[xx, yy], preferred_element_type=F32)

    order = (4, 3, 5, 2, 6, 1, 7, 0)
    for d in order:
        yy = lax.rem(y + d, NY)
        for e in (2, 1, 3):
            xx = lax.rem(x + e, NX)
            x_out[e - 1, d] = weighted(xx, yy).astype(BF16)
            remote(
                x_out.at[e - 1, d], x_in.at[e - 1, d], xs.at[e - 1, d], xr.at[e - 1, d], device(xx, y, z, core)
            ).start()
    for d in order:
        own[d] = weighted(x, lax.rem(y + d, NY))

    for d in order:
        for e in range(3):
            arrived(x_in.at[e, d], xr.at[e, d])
        block = own[d] + x_in[0, d].astype(F32) + x_in[1, d].astype(F32) + x_in[2, d].astype(F32)
        if d:
            y_out[d - 1] = block.astype(BF16)
            remote(
                y_out.at[d - 1], y_in.at[d - 1], ys.at[d - 1], yr.at[d - 1], device(x, lax.rem(y + d, NY), z, core)
            ).start()
    for d in range(7):
        arrived(y_in.at[d], yr.at[d])
        block = block + y_in[d].astype(F32)
    z_out[...] = block

    t_copies = [
        remote(z_out, total_in.at[z], ts.at[d], tr.at[z], device(x, y, 2 * lax.rem(zh + d, 4) + core, core))
        for d in range(4)
    ]
    for copy in t_copies[1:]:
        copy.start()

    @pl.when(core == zl)
    def _():
        total_in[z] = z_out[...]

    @pl.when(core != zl)
    def _():
        t_copies[0].start()

    total_copy = remote(total, total, core_send.at[3], core_recv.at[3], partner)

    @pl.when(core == zl)
    def _():
        for d in range(1, NZ):
            s = lax.rem(z + d, NZ)
            arrived(total_in.at[s], tr.at[s])
        value = total_in[0]
        for s in range(1, NZ):
            value = value + total_in[s]
        total[...] = value
        total_copy.start()

    @pl.when(core != zl)
    def _():
        total_copy.wait_recv()

    for t in range(TILES):
        tile = slice(t * LANES, (t + 1) * LANES)
        rows = total[:, tile]
        for h in range(2):
            value = tent[0, :, tile] * rows[h * 8 : h * 8 + 1, :]
            for o in range(1, ORIENTS):
                value = value + tent[o, :, tile] * rows[h * 8 + o : h * 8 + o + 1, :]
            volume_out[h, :, tile] = value

    left(part.at[far], core_send.at[0])
    left(meta.at[core], core_send.at[1])
    left(logit, core_send.at[2])
    for q in range(4):
        raw_copies[q].wait_send()
    for d in range(1, NZ):
        left(own_half, zs.at[d])
    for d in range(1, NY):
        left(slices.at[x * NY + y], ag_ys.at[d])
    for d in range(NY):
        for e in range(3):
            left(slices.at[x * NY + lax.rem(y + d, NY)], ag_xs.at[e, d])
            left(x_out.at[e, d], xs.at[e, d])
    for d in range(7):
        left(y_out.at[d], ys.at[d])
    for d in range(1, 4):
        left(z_out, ts.at[d])

    @pl.when(core != zl)
    def _():
        left(own_half, zs.at[0])
        left(z_out, ts.at[0])

    @pl.when(core == zl)
    def _():
        left(total, core_send.at[3])


def body(particle_data, optics_label, half_set, shift_offset, ctf_bank, noise_power, half_maps, orient_index):
    dma = pltpu.SemaphoreType.DMA
    smem = pl.BlockSpec(memory_space=pltpu.SMEM)
    vmem = pl.BlockSpec(memory_space=pltpu.VMEM)
    anywhere = pl.BlockSpec(memory_space=pl.ANY)
    log_total, volume = pl.pallas_call(
        kernel,
        out_shape=(
            jax.ShapeDtypeStruct((1, MINE), F32),
            jax.ShapeDtypeStruct((2, PLANES, BLOCK), F32),
        ),
        in_specs=[smem, smem, smem, smem, vmem, anywhere, anywhere, anywhere],
        out_specs=(vmem, vmem),
        scratch_shapes=[
            pltpu.VMEM((ORIENTS, PLANES, BLOCK), F32),
            pltpu.VMEM((2, ORIENTS, BLOCK), F32),
            pltpu.VMEM((ORIENTS, BLOCK), F32),
            pltpu.VMEM((ORIENTS, BLOCK), F32),
            pltpu.VMEM((8, ORIENTS, BLOCK), F32),
            pltpu.VMEM((NX * NY, ROWS, BLOCK), BF16),
            pltpu.VMEM((2, 4, MINE, CHUNK), BF16),
            pltpu.VMEM((2, 4, MINE, LANES), jnp.int32),
            pltpu.VMEM((2, GROUPS, CHUNK), F32),
            pltpu.VMEM((2, 1, CHUNK), F32),
            pltpu.VMEM((2 * NY, GROUPS, BLOCK), F32),
            pltpu.VMEM((40, 2, PAIR, LANES), F32),
            pltpu.VMEM((2, 2, PAIR, LANES), F32),
            pltpu.VMEM((NX, NY, PAIR, BLOCK), BF16),
            pltpu.VMEM((ROWS, LANES), F32),
            pltpu.VMEM((ROWS, LANES), F32),
            pltpu.VMEM((ORIENTS, LANES), F32),
            pltpu.VMEM((ORIENTS, LANES), F32),
            pltpu.VMEM((ROWS, LANES), BF16),
            pltpu.VMEM((3, NY, ROWS, BLOCK), BF16),
            pltpu.VMEM((3, NY, ROWS, BLOCK), BF16),
            pltpu.VMEM((NY, ROWS, BLOCK), F32),
            pltpu.VMEM((7, ROWS, BLOCK), BF16),
            pltpu.VMEM((7, ROWS, BLOCK), BF16),
            pltpu.VMEM((ROWS, BLOCK), F32),
            pltpu.VMEM((NZ, ROWS, BLOCK), F32),
            pltpu.VMEM((ROWS, BLOCK), F32),
            dma((8,)),
            dma((4,)),
            dma((4,)),
            dma((4,)),
            dma((4,)),
            dma((8,)),
            dma((8,)),
            dma((8,)),
            dma((3, 8)),
            dma((NX * NY,)),
            dma((3, 8)),
            dma((3, 8)),
            dma((7,)),
            dma((7,)),
            dma((4,)),
            dma((8,)),
        ],
        compiler_params=pltpu.CompilerParams(
            collective_id=0, has_side_effects=True, vmem_limit_bytes=40 * 1024 * 1024
        ),
        name="score_and_insert",
    )(
        orient_index, optics_label, half_set, shift_offset, half_maps, particle_data, ctf_bank,
        noise_power.reshape(1, PIX),
    )
    return log_total.reshape(MINE), volume


def solution(mesh):
    placed = (
        P(("slab", "work"), None),
        P(("slab", "work")),
        P(("slab", "work")),
        P(("slab", "work"), None),
        P(),
        P(),
        P(None, "slab", "work"),
        P(),
    )
    return jax.shard_map(
        body,
        mesh=mesh,
        in_specs=placed,
        out_specs=(P(("slab", "work")), P(None, "slab", "work")),
        check_vma=False,
    )
```

```python
import math

import jax
import jax.numpy as jnp
from jax import lax
from jax.experimental import pallas as pl
from jax.experimental.pallas import tpu as pltpu
from jax.sharding import PartitionSpec as P

ORDER = 256
PIX = 20480
GRID = 4608
GROUPS = 8
ORIENTS = 8
NX, NY, NZ = 4, 8, 8
PLANES = 32
BLOCK = 640
CHUNK = NY * BLOCK
ROWS = 2 * ORIENTS
MINE = 16
LANES = 128
TILES = BLOCK // LANES
MESH = pl.DeviceIdType.MESH
F32 = jnp.float32
BF16 = jnp.bfloat16


def device(x, y, z, core):
    return {
        "slab": lax.div(z, 2) * 2 + core,
        "work": (x * 2 + lax.rem(z, 2)) * NY + y,
    }


def turn_of(steps):
    k = lax.bitwise_and(steps, 255)
    quadrant = lax.shift_right_logical(k + 32, 6)
    r = (k - 64 * quadrant).astype(F32) * F32(2.0 * math.pi / ORDER)
    r2 = r * r
    s = r * (1.0 + r2 * (-1.0 / 6 + r2 * (1.0 / 120 + r2 * (-1.0 / 5040 + r2 * (1.0 / 362880)))))
    c = 1.0 + r2 * (-0.5 + r2 * (1.0 / 24 + r2 * (-1.0 / 720 + r2 * (1.0 / 40320 - r2 * (1.0 / 3628800)))))
    odd = lax.bitwise_and(quadrant, 1) == 1
    low = jnp.where(odd, s, c)
    high = jnp.where(odd, c, s)
    turned = lax.bitwise_and(quadrant, 3)
    cosine = jnp.where((turned == 1) | (turned == 2), -low, low)
    sine = jnp.where(turned >= 2, -high, high)
    return cosine, -sine


def tents_of(orient, slab, work):
    row = lax.broadcasted_iota(jnp.int32, (ORIENTS, LANES), 0)
    index = jnp.zeros((ORIENTS, LANES), jnp.int32)
    for o in range(ORIENTS):
        index = jnp.where(row == o, orient[o], index)
    sines = jnp.sin(math.pi * (index.astype(F32) + 0.5) / GRID - 0.5 * math.pi)
    plane = (slab * PLANES + lax.broadcasted_iota(jnp.int32, (PLANES, LANES), 0)).astype(F32)
    lane = lax.broadcasted_iota(jnp.int32, (1, LANES), 1)

    def tents(t, o):
        coord_v = (lane - LANES + LANES * lax.rem(work + t, 2)).astype(F32)
        depth = ORDER // 2 + sines[o : o + 1, :] * coord_v
        return jnp.maximum(0.0, 1.0 - jnp.abs(plane - depth))

    return tents


def kernel(
    orient_in, label_in, half_in, shift_in, maps_in, data_in, ctf_in, noise_in,
    log_out, total,
    orient, label, half, shift, maps, data, ctf, noise,
    part, swap, own_half, z_in, slices, meta, square, turn_u, turn_v, staged, prep,
    logit, logit_in, weight, own, y_out, y_in, z_out, total_in,
    local_sem, core_send, core_recv, ms, mr, ps, pr, zs, zr, ag_s, ag_r, ls, lr, ys, yr, ts, tr,
):
    slab = lax.axis_index("slab")
    work = lax.axis_index("work")
    core = lax.rem(slab, 2)
    zh = lax.div(slab, 2)
    x = lax.div(work, 2 * NY)
    zl = lax.rem(lax.div(work, NY), 2)
    y = lax.rem(work, NY)
    z = 2 * zh + zl
    far = 1 - core
    partner = device(x, y, z, far)
    piece = 2 * x + core

    def remote(src, dst, send, recv, target):
        return pltpu.make_async_remote_copy(
            src_ref=src, dst_ref=dst, send_sem=send, recv_sem=recv, device_id=target, device_id_type=MESH
        )

    def arrived(dst, recv):
        remote(dst, dst, recv, recv, partner).wait_recv()

    def left(src, send):
        remote(src, src, send, send, partner).wait_send()

    def along_x(d):
        q = lax.rem(piece + d, 2 * NX)
        return device(lax.div(q, 2), y, z, lax.rem(q, 2))

    barrier = pltpu.get_barrier_semaphore()
    friends = [along_x(d) for d in range(1, 2 * NX)]
    friends += [device(x, y, lax.rem(z + d, NZ), k) for d in range(1, NZ) for k in range(2)]
    friends += [device(x, lax.rem(y + d, NY), z, core) for d in range(1, NY)]
    for friend in friends:
        pl.semaphore_signal(barrier, inc=1, device_id=friend, device_id_type=MESH)

    pairs = [
        (orient_in, orient), (maps_in, maps), (label_in, label), (half_in, half), (shift_in, shift),
        (data_in, data), (ctf_in, ctf), (noise_in, noise),
    ]
    local = [pltpu.make_async_copy(src, dst, local_sem.at[i]) for i, (src, dst) in enumerate(pairs)]
    for copy in local:
        copy.start()

    local[0].wait()
    local[1].wait()
    tents = tents_of(orient, slab, work)
    for t in range(TILES):
        tile = slice(t * LANES, (t + 1) * LANES)
        values = [maps[h, :, tile].astype(F32) for h in range(2)]
        found = [[], []]
        for o in range(ORIENTS):
            near = tents(t, o)
            for h in range(2):
                found[h].append(jnp.sum(near * values[h], axis=0, keepdims=True))
        for h in range(2):
            part[h, :, tile] = jnp.concatenate(found[h], axis=0)

    pl.semaphore_wait(barrier, len(friends))

    swap_copy = remote(part.at[far], swap, core_send.at[0], core_recv.at[0], partner)
    swap_copy.start()

    for copy in local[2:5]:
        copy.wait()
    row8 = lax.broadcasted_iota(jnp.int32, (ORIENTS, LANES), 0)
    lane8 = lax.broadcasted_iota(jnp.int32, (ORIENTS, LANES), 1)
    row16 = lax.broadcasted_iota(jnp.int32, (MINE, LANES), 0)
    lane16 = lax.broadcasted_iota(jnp.int32, (MINE, LANES), 1)
    about = [jnp.zeros((MINE, LANES), jnp.int32) for _ in range(3)]
    across = jnp.zeros((ORIENTS, LANES), jnp.int32)
    for i in range(MINE):
        here = row16 == i
        about[0] = jnp.where(here, label[i], about[0])
        about[1] = jnp.where(here, shift[0, i], about[1])
        about[2] = jnp.where(here, shift[1, i], about[2])
        there = lane8 == piece * MINE + i
        across = jnp.where(there, jnp.where(row8 == 0, label[i], half[i]), across)
    meta[piece] = across
    meta_copies = [remote(meta.at[piece], meta.at[piece], ms.at[d - 1], mr.at[piece], along_x(d)) for d in range(1, 8)]

    for v in range(2):
        cosine, sine = turn_of((lane16 + (v - 1) * LANES) * about[2])
        turn_v[v, 0] = cosine
        turn_v[v, 1] = sine
    cosine, sine = turn_of(lane16 * about[1])
    for u in range(PIX // ORDER):
        turn_u[u, 0] = jnp.broadcast_to(cosine[:, u : u + 1], (MINE, LANES))
        turn_u[u, 1] = jnp.broadcast_to(sine[:, u : u + 1], (MINE, LANES))
    bits = [lax.bitwise_and(about[0], 1 << j) != 0 for j in range(3)]

    swap_copy.wait_recv()
    own_half[...] = part[core] + swap[...]
    z_copies = [
        remote(own_half, z_in.at[slab], zs.at[d], zr.at[slab], device(x, y, lax.rem(z + d, NZ), zl))
        for d in range(NZ)
    ]
    for d in (4, 3, 5, 2, 6, 1, 7):
        z_copies[d].start()

    @pl.when(core == zl)
    def _():
        z_in[slab] = own_half[...]

    @pl.when(core != zl)
    def _():
        z_copies[0].start()

    for copy in local[5:]:
        copy.wait()

    def prepare(q, k, keep):
        def step(pair, carry):
            span = pl.ds(pl.multiple_of(q * (2 * CHUNK) + k * CHUNK + pair * (2 * BLOCK), LANES), 2 * BLOCK)
            imag_span = pl.ds(pl.multiple_of(PIX + q * (2 * CHUNK) + k * CHUNK + pair * (2 * BLOCK), LANES), 2 * BLOCK)
            filters = ctf[:, span]
            variance = noise[:, span]
            scaled = filters / variance
            real_rows = data[:, span]
            imag_rows = data[:, imag_span]
            if keep:
                squared = filters * filters / variance
            for t in range(2 * TILES):
                tile = slice(t * LANES, (t + 1) * LANES)
                if keep:
                    square[pair * 2 + t // TILES, :, (t % TILES) * LANES : (t % TILES + 1) * LANES] = squared[:, tile]
                wide = [jnp.broadcast_to(scaled[g : g + 1, tile], (MINE, LANES)) for g in range(GROUPS)]
                wide = [jnp.where(bits[0], wide[2 * j + 1], wide[2 * j]) for j in range(4)]
                wide = [jnp.where(bits[1], wide[2 * j + 1], wide[2 * j]) for j in range(2)]
                factor = jnp.where(bits[2], wide[1], wide[0])
                u = (2 * q + k) * (CHUNK // ORDER) + pair * 5 + t // 2
                cos_u, sin_u, cos_v, sin_v = turn_u[u, 0], turn_u[u, 1], turn_v[t % 2, 0], turn_v[t % 2, 1]
                cos_q = cos_u * cos_v - sin_u * sin_v
                sin_q = sin_u * cos_v + cos_u * sin_v
                real = real_rows[:, tile].astype(F32)
                imag = imag_rows[:, tile].astype(F32)
                place = pl.ds(pl.multiple_of(pair * (2 * BLOCK) + t * LANES, LANES), LANES)
                staged[2 * q + k, :, place] = ((real * cos_q - imag * sin_q) * factor).astype(BF16)
                staged[2 * (q + 2) + k, :, place] = ((real * sin_q + imag * cos_q) * factor).astype(BF16)
            return carry

        lax.fori_loop(0, NY // 2, step, 0)

    parity = lax.rem(x, 2)

    def part_copy(e, k):
        xx = lax.rem(x + e, NX)
        slot = 2 * e + (0 if k is core else 1)
        return remote(staged.at[2 * xx + k], prep.at[piece], ps.at[slot], pr.at[piece], device(xx, y, z, k))

    for steps, k, dests in (((1, far, (1, 3)), (0, far, (2, 0)), (1, core, (1, 3)), (0, core, (2,)))):
        q = lax.rem(parity + steps, 2)
        prepare(q, k, steps == 0 and k is core)
        for e in dests:
            part_copy(e, k).start()
    keep_copy = pltpu.make_async_copy(staged.at[piece], prep.at[piece], ps.at[0])
    keep_copy.start()
    for copy in meta_copies:
        copy.start()

    for d in range(1, 8):
        s = lax.rem(slab + d, 8)
        arrived(z_in.at[s], zr.at[s])

    @pl.when(core != zl)
    def _():
        arrived(z_in.at[slab], zr.at[slab])

    halves = [z_in[h] + z_in[2 + h] + z_in[4 + h] + z_in[6 + h] for h in range(2)]
    slices[y] = jnp.concatenate(halves, axis=0).astype(BF16)

    for d in (4, 3, 5, 2, 6, 1, 7):
        remote(
            slices.at[y], slices.at[y], ag_s.at[d - 1], ag_r.at[y], device(x, lax.rem(y + d, NY), z, core)
        ).start()

    sums = [jnp.zeros((ROWS, LANES), F32) for _ in range(GROUPS)]
    for d in (0, 1, 7, 2, 6, 3, 5, 4):
        yy = lax.rem(y + d, NY)
        if d:
            arrived(slices.at[yy], ag_r.at[yy])
        for t in range(TILES):
            tile = slice(t * LANES, (t + 1) * LANES)
            rows = slices[yy, :, tile].astype(F32)
            size = rows * rows
            gain = square[yy, :, tile]
            for g in range(GROUPS):
                sums[g] = sums[g] + size * gain[g : g + 1, :]
    for d in range(1, 8):
        p = lax.rem(piece + d, 8)
        arrived(meta.at[p], mr.at[p])
    about_lanes = meta[0]
    for p in range(1, 8):
        about_lanes = about_lanes + meta[p]
    label_lane = about_lanes[0:1, :]
    half_lane = about_lanes[1:2, :]
    penalty = jnp.zeros((ROWS, LANES), F32)
    for g in range(GROUPS):
        power = jnp.sum(sums[g], axis=1, keepdims=True)
        penalty = penalty + jnp.where(label_lane == g, 0.5 * power, 0.0)

    keep_copy.wait()
    for d in range(1, 8):
        p = lax.rem(piece + d, 8)
        arrived(prep.at[p], pr.at[p])
    cross = jnp.zeros((ROWS, LANES), F32)
    for b in range(NY):
        rows = prep[:, :, b * BLOCK : (b + 1) * BLOCK].reshape(LANES, BLOCK)
        cross = cross + lax.dot_general(slices[b], rows, (((1,), (1,)), ((), ())), preferred_element_type=F32)
    value = cross - penalty
    logit[...] = jnp.where(half_lane == 0, value[0:8, :], value[8:16, :])
    for d in range(1, 8):
        remote(logit, logit_in.at[piece], ls.at[d - 1], lr.at[piece], along_x(d)).start()
    logit_in[piece] = logit[...]
    for d in range(1, 8):
        p = lax.rem(piece + d, 8)
        arrived(logit_in.at[p], lr.at[p])
    logits = logit_in[0]
    for p in range(1, 8):
        logits = logits + logit_in[p]
    highest = jnp.max(logits, axis=0, keepdims=True)
    log_total = highest + jnp.log(jnp.sum(jnp.exp(logits - highest), axis=0, keepdims=True))
    weights = jnp.exp(logits - log_total)
    both = [jnp.where(half_lane == h, weights, 0.0) for h in range(2)]
    weight[...] = jnp.concatenate(both, axis=0).astype(BF16)
    shares = weight[...]

    def weighted(yy):
        span = pl.ds(pl.multiple_of(yy * BLOCK, LANES), BLOCK)
        return jnp.dot(shares, prep[:, :, span].reshape(LANES, BLOCK), preferred_element_type=F32)

    for d in (4, 3, 5, 2, 6, 1, 7):
        yy = lax.rem(y + d, NY)
        y_out[d - 1] = weighted(yy).astype(BF16)
        remote(
            y_out.at[d - 1], y_in.at[d - 1], ys.at[d - 1], yr.at[d - 1], device(x, yy, z, core)
        ).start()
    block = weighted(y)
    lane_sets = [log_total[:, p * MINE : (p + 1) * MINE] for p in range(8)]
    chosen = lane_sets[0]
    for p in range(1, 8):
        chosen = jnp.where(piece == p, lane_sets[p], chosen)
    log_out[...] = chosen
    for d in (0, 6, 1, 5, 2, 4, 3):
        arrived(y_in.at[d], yr.at[d])
        block = block + y_in[d].astype(F32)
    own[...] = block
    z_out[...] = block.astype(BF16)

    t_copies = [
        remote(z_out, total_in.at[z], ts.at[d], tr.at[z], device(x, y, 2 * lax.rem(zh + d, 4) + core, core))
        for d in range(4)
    ]
    for d in (2, 1, 3):
        t_copies[d].start()

    @pl.when(core != zl)
    def _():
        t_copies[0].start()

    total_copy = remote(total, total, core_send.at[1], core_recv.at[1], partner)

    @pl.when(core == zl)
    def _():
        value = own[...]
        for d in (1, 7, 2, 6, 3, 5, 4):
            s = lax.rem(z + d, NZ)
            arrived(total_in.at[s], tr.at[s])
            value = value + total_in[s].astype(F32)
        total[...] = value
        total_copy.start()

    @pl.when(core != zl)
    def _():
        total_copy.wait_recv()

    left(part.at[far], core_send.at[0])
    for d in range(7):
        left(meta.at[piece], ms.at[d])
        left(slices.at[y], ag_s.at[d])
        left(logit, ls.at[d])
        left(y_out.at[d], ys.at[d])
        left(own_half, zs.at[d + 1])
        left(staged.at[d], ps.at[d + 1])
    for d in range(1, 4):
        left(z_out, ts.at[d])

    @pl.when(core != zl)
    def _():
        left(own_half, zs.at[0])
        left(z_out, ts.at[0])

    @pl.when(core == zl)
    def _():
        left(total, core_send.at[1])


def insert_kernel(orient, total, log_in, log_out, volume_out):
    tents = tents_of(orient, lax.axis_index("slab"), lax.axis_index("work"))
    log_out[...] = log_in[...]
    for t in range(TILES):
        tile = slice(t * LANES, (t + 1) * LANES)
        rows = total[:, tile]
        found = [jnp.zeros((PLANES, LANES), F32) for _ in range(2)]
        for o in range(ORIENTS):
            near = tents(t, o)
            for h in range(2):
                found[h] = found[h] + near * rows[h * ORIENTS + o : h * ORIENTS + o + 1, :]
        for h in range(2):
            volume_out[h, :, tile] = found[h]


def body(particle_data, optics_label, half_set, shift_offset, ctf_bank, noise_power, half_maps, orient_index):
    dma = pltpu.SemaphoreType.DMA
    smem = pl.BlockSpec(memory_space=pltpu.SMEM)
    vmem = pl.BlockSpec(memory_space=pltpu.VMEM)
    anywhere = pl.BlockSpec(memory_space=pl.ANY)
    log_total, total = pl.pallas_call(
        kernel,
        out_shape=(
            jax.ShapeDtypeStruct((1, MINE), F32),
            jax.ShapeDtypeStruct((ROWS, BLOCK), F32),
        ),
        in_specs=[anywhere] * 8,
        out_specs=(vmem, vmem),
        scratch_shapes=[
            pltpu.SMEM((ORIENTS,), jnp.int32),
            pltpu.SMEM((MINE,), jnp.int32),
            pltpu.SMEM((MINE,), jnp.int32),
            pltpu.SMEM((2, MINE), jnp.int32),
            pltpu.VMEM((2, PLANES, BLOCK), BF16),
            pltpu.VMEM((MINE, 2 * PIX), BF16),
            pltpu.VMEM((GROUPS, PIX), F32),
            pltpu.VMEM((1, PIX), F32),
            pltpu.VMEM((2, ORIENTS, BLOCK), F32),
            pltpu.VMEM((ORIENTS, BLOCK), F32),
            pltpu.VMEM((ORIENTS, BLOCK), F32),
            pltpu.VMEM((8, ORIENTS, BLOCK), F32),
            pltpu.VMEM((NY, ROWS, BLOCK), BF16),
            pltpu.VMEM((8, ORIENTS, LANES), jnp.int32),
            pltpu.VMEM((NY, GROUPS, BLOCK), F32),
            pltpu.VMEM((PIX // ORDER, 2, MINE, LANES), F32),
            pltpu.VMEM((2, 2, MINE, LANES), F32),
            pltpu.VMEM((8, MINE, CHUNK), BF16),
            pltpu.VMEM((8, MINE, CHUNK), BF16),
            pltpu.VMEM((ORIENTS, LANES), F32),
            pltpu.VMEM((8, ORIENTS, LANES), F32),
            pltpu.VMEM((ROWS, LANES), BF16),
            pltpu.VMEM((ROWS, BLOCK), F32),
            pltpu.VMEM((7, ROWS, BLOCK), BF16),
            pltpu.VMEM((7, ROWS, BLOCK), BF16),
            pltpu.VMEM((ROWS, BLOCK), BF16),
            pltpu.VMEM((NZ, ROWS, BLOCK), BF16),
            dma((8,)),
            dma((2,)),
            dma((2,)),
            dma((7,)),
            dma((8,)),
            dma((8,)),
            dma((8,)),
            dma((8,)),
            dma((8,)),
            dma((7,)),
            dma((8,)),
            dma((7,)),
            dma((8,)),
            dma((7,)),
            dma((7,)),
            dma((4,)),
            dma((8,)),
        ],
        compiler_params=pltpu.CompilerParams(
            collective_id=0, has_side_effects=True, vmem_limit_bytes=64 * 1024 * 1024
        ),
        name="score_and_insert",
    )(
        orient_index, optics_label, half_set, shift_offset.T, half_maps, particle_data, ctf_bank,
        noise_power.reshape(1, PIX),
    )
    log_total, volume = pl.pallas_call(
        insert_kernel,
        out_shape=(
            jax.ShapeDtypeStruct((1, MINE), F32),
            jax.ShapeDtypeStruct((2, PLANES, BLOCK), F32),
        ),
        in_specs=[smem, vmem, vmem],
        out_specs=(vmem, vmem),
        name="insert",
    )(orient_index, total, log_total)
    return log_total.reshape(MINE), volume


def solution(mesh):
    placed = (
        P(("slab", "work"), None),
        P(("slab", "work")),
        P(("slab", "work")),
        P(("slab", "work"), None),
        P(),
        P(),
        P(None, "slab", "work"),
        P(),
    )
    return jax.shard_map(
        body,
        mesh=mesh,
        in_specs=placed,
        out_specs=(P(("slab", "work")), P(None, "slab", "work")),
        check_vma=False,
    )
```

```python
import math

import jax
import jax.numpy as jnp
from jax import lax
from jax.experimental import pallas as pl
from jax.experimental.pallas import tpu as pltpu
from jax.sharding import PartitionSpec as P

ORDER = 256
PIX = 20480
GRID = 4608
GROUPS = 8
ORIENTS = 8
NX, NY, NZ = 4, 8, 8
PLANES = 32
BLOCK = 640
CHUNK = NY * BLOCK
ROWS = 2 * ORIENTS
MINE = 16
LANES = 128
TILES = BLOCK // LANES
MESH = pl.DeviceIdType.MESH
F32 = jnp.float32
BF16 = jnp.bfloat16


def device(x, y, z, core):
    return {
        "slab": lax.div(z, 2) * 2 + core,
        "work": (x * 2 + lax.rem(z, 2)) * NY + y,
    }


def turn_of(steps):
    k = lax.bitwise_and(steps, 255)
    quadrant = lax.shift_right_logical(k + 32, 6)
    r = (k - 64 * quadrant).astype(F32) * F32(2.0 * math.pi / ORDER)
    r2 = r * r
    s = r * (1.0 + r2 * (-1.0 / 6 + r2 * (1.0 / 120 + r2 * (-1.0 / 5040 + r2 * (1.0 / 362880)))))
    c = 1.0 + r2 * (-0.5 + r2 * (1.0 / 24 + r2 * (-1.0 / 720 + r2 * (1.0 / 40320 - r2 * (1.0 / 3628800)))))
    odd = lax.bitwise_and(quadrant, 1) == 1
    low = jnp.where(odd, s, c)
    high = jnp.where(odd, c, s)
    turned = lax.bitwise_and(quadrant, 3)
    cosine = jnp.where((turned == 1) | (turned == 2), -low, low)
    sine = jnp.where(turned >= 2, -high, high)
    return cosine, -sine


def tents_of(orient, slab, work):
    row = lax.broadcasted_iota(jnp.int32, (ORIENTS, LANES), 0)
    index = jnp.zeros((ORIENTS, LANES), jnp.int32)
    for o in range(ORIENTS):
        index = jnp.where(row == o, orient[o], index)
    sines = jnp.sin(math.pi * (index.astype(F32) + 0.5) / GRID - 0.5 * math.pi)
    plane = (slab * PLANES + lax.broadcasted_iota(jnp.int32, (PLANES, LANES), 0)).astype(F32)
    lane = lax.broadcasted_iota(jnp.int32, (1, LANES), 1)

    def tents(t, o):
        coord_v = (lane - LANES + LANES * lax.rem(work + t, 2)).astype(F32)
        depth = ORDER // 2 + sines[o : o + 1, :] * coord_v
        return jnp.maximum(0.0, 1.0 - jnp.abs(plane - depth))

    return tents


def kernel(
    orient_in, label_in, half_in, shift_in, maps_in, data_in, ctf_in, noise_in,
    log_out, total,
    orient, label, half, shift, maps, data, ctf, noise,
    part, swap, own_half, z_in, slices, meta, square, turn_u, turn_v, staged, prep,
    logit, logit_in, weight, own, y_out, y_in, z_out, total_in,
    local_sem, core_send, core_recv, ms, mr, ps, pr, zs, zr, ag_s, ag_r, ls, lr, ys, yr, ts, tr,
):
    slab = lax.axis_index("slab")
    work = lax.axis_index("work")
    core = lax.rem(slab, 2)
    zh = lax.div(slab, 2)
    x = lax.div(work, 2 * NY)
    zl = lax.rem(lax.div(work, NY), 2)
    y = lax.rem(work, NY)
    z = 2 * zh + zl
    far = 1 - core
    partner = device(x, y, z, far)
    piece = 2 * x + core

    def remote(src, dst, send, recv, target):
        return pltpu.make_async_remote_copy(
            src_ref=src, dst_ref=dst, send_sem=send, recv_sem=recv, device_id=target, device_id_type=MESH
        )

    def arrived(dst, recv):
        remote(dst, dst, recv, recv, partner).wait_recv()

    def left(src, send):
        remote(src, src, send, send, partner).wait_send()

    def along_x(d):
        q = lax.rem(piece + d, 2 * NX)
        return device(lax.div(q, 2), y, z, lax.rem(q, 2))

    barrier = pltpu.get_barrier_semaphore()
    friends = [along_x(d) for d in range(1, 2 * NX)]
    friends += [device(x, y, lax.rem(z + d, NZ), k) for d in range(1, NZ) for k in range(2)]
    friends += [device(x, lax.rem(y + d, NY), z, core) for d in range(1, NY)]
    for friend in friends:
        pl.semaphore_signal(barrier, inc=1, device_id=friend, device_id_type=MESH)

    pairs = [
        (orient_in, orient), (maps_in, maps), (label_in, label), (half_in, half), (shift_in, shift),
        (data_in, data), (ctf_in, ctf), (noise_in, noise),
    ]
    local = [pltpu.make_async_copy(src, dst, local_sem.at[i]) for i, (src, dst) in enumerate(pairs)]
    for copy in local:
        copy.start()

    local[0].wait()
    local[1].wait()
    tents = tents_of(orient, slab, work)
    for t in range(TILES):
        tile = slice(t * LANES, (t + 1) * LANES)
        values = [maps[h, :, tile].astype(F32) for h in range(2)]
        found = [[], []]
        for o in range(ORIENTS):
            near = tents(t, o)
            for h in range(2):
                found[h].append(jnp.sum(near * values[h], axis=0, keepdims=True))
        for h in range(2):
            part[h, :, tile] = jnp.concatenate(found[h], axis=0)

    for copy in local[2:5]:
        copy.wait()
    row8 = lax.broadcasted_iota(jnp.int32, (ORIENTS, LANES), 0)
    lane8 = lax.broadcasted_iota(jnp.int32, (ORIENTS, LANES), 1)
    row16 = lax.broadcasted_iota(jnp.int32, (MINE, LANES), 0)
    lane16 = lax.broadcasted_iota(jnp.int32, (MINE, LANES), 1)
    about = [jnp.zeros((MINE, LANES), jnp.int32) for _ in range(3)]
    across = jnp.zeros((ORIENTS, LANES), jnp.int32)
    for i in range(MINE):
        here = row16 == i
        about[0] = jnp.where(here, label[i], about[0])
        about[1] = jnp.where(here, shift[0, i], about[1])
        about[2] = jnp.where(here, shift[1, i], about[2])
        there = lane8 == piece * MINE + i
        across = jnp.where(there, jnp.where(row8 == 0, label[i], half[i]), across)
    meta[piece] = across
    meta_copies = [remote(meta.at[piece], meta.at[piece], ms.at[d - 1], mr.at[piece], along_x(d)) for d in range(1, 8)]

    for v in range(2):
        cosine, sine = turn_of((lane16 + (v - 1) * LANES) * about[2])
        turn_v[v, 0] = cosine
        turn_v[v, 1] = sine
    cosine, sine = turn_of(lane16 * about[1])
    for u in range(PIX // ORDER):
        turn_u[u, 0] = jnp.broadcast_to(cosine[:, u : u + 1], (MINE, LANES))
        turn_u[u, 1] = jnp.broadcast_to(sine[:, u : u + 1], (MINE, LANES))
    bits = [lax.bitwise_and(about[0], 1 << j) != 0 for j in range(3)]

    for copy in local[5:]:
        copy.wait()

    def prepare(q, k, keep):
        def step(pair, carry):
            span = pl.ds(pl.multiple_of(q * (2 * CHUNK) + k * CHUNK + pair * (2 * BLOCK), LANES), 2 * BLOCK)
            imag_span = pl.ds(pl.multiple_of(PIX + q * (2 * CHUNK) + k * CHUNK + pair * (2 * BLOCK), LANES), 2 * BLOCK)
            filters = ctf[:, span]
            variance = noise[:, span]
            scaled = filters / variance
            real_rows = data[:, span]
            imag_rows = data[:, imag_span]
            if keep:
                squared = filters * filters / variance
            for t in range(2 * TILES):
                tile = slice(t * LANES, (t + 1) * LANES)
                if keep:
                    square[pair * 2 + t // TILES, :, (t % TILES) * LANES : (t % TILES + 1) * LANES] = squared[:, tile]
                wide = [jnp.broadcast_to(scaled[g : g + 1, tile], (MINE, LANES)) for g in range(GROUPS)]
                wide = [jnp.where(bits[0], wide[2 * j + 1], wide[2 * j]) for j in range(4)]
                wide = [jnp.where(bits[1], wide[2 * j + 1], wide[2 * j]) for j in range(2)]
                factor = jnp.where(bits[2], wide[1], wide[0])
                u = (2 * q + k) * (CHUNK // ORDER) + pair * 5 + t // 2
                cos_u, sin_u, cos_v, sin_v = turn_u[u, 0], turn_u[u, 1], turn_v[t % 2, 0], turn_v[t % 2, 1]
                cos_q = cos_u * cos_v - sin_u * sin_v
                sin_q = sin_u * cos_v + cos_u * sin_v
                real = real_rows[:, tile].astype(F32)
                imag = imag_rows[:, tile].astype(F32)
                place = pl.ds(pl.multiple_of(pair * (2 * BLOCK) + t * LANES, LANES), LANES)
                staged[2 * q + k, :, place] = ((real * cos_q - imag * sin_q) * factor).astype(BF16)
                staged[2 * (q + 2) + k, :, place] = ((real * sin_q + imag * cos_q) * factor).astype(BF16)
            return carry

        lax.fori_loop(0, NY // 2, step, 0)

    parity = lax.rem(x, 2)

    def part_copy(e, k):
        xx = lax.rem(x + e, NX)
        slot = 2 * e + (0 if k is core else 1)
        return remote(staged.at[2 * xx + k], prep.at[piece], ps.at[slot], pr.at[piece], device(xx, y, z, k))

    for steps, k in ((1, far), (0, far), (1, core), (0, core)):
        prepare(lax.rem(parity + steps, 2), k, steps == 0 and k is core)

    pl.semaphore_wait(barrier, len(friends))

    swap_copy = remote(part.at[far], swap, core_send.at[0], core_recv.at[0], partner)
    swap_copy.start()

    for k in (far, core):
        for e in (1, 2, 3):
            part_copy(e, k).start()
    part_copy(0, far).start()
    keep_copy = pltpu.make_async_copy(staged.at[piece], prep.at[piece], ps.at[0])
    keep_copy.start()
    for copy in meta_copies:
        copy.start()

    swap_copy.wait_recv()
    own_half[...] = part[core] + swap[...]
    z_copies = [
        remote(own_half, z_in.at[slab], zs.at[d], zr.at[slab], device(x, y, lax.rem(z + d, NZ), zl))
        for d in range(NZ)
    ]
    for d in (4, 3, 5, 2, 6, 1, 7):
        z_copies[d].start()

    @pl.when(core == zl)
    def _():
        z_in[slab] = own_half[...]

    @pl.when(core != zl)
    def _():
        z_copies[0].start()

    for d in range(1, 8):
        s = lax.rem(slab + d, 8)
        arrived(z_in.at[s], zr.at[s])

    @pl.when(core != zl)
    def _():
        arrived(z_in.at[slab], zr.at[slab])

    halves = [z_in[h] + z_in[2 + h] + z_in[4 + h] + z_in[6 + h] for h in range(2)]
    slices[y] = jnp.concatenate(halves, axis=0).astype(BF16)

    for d in (4, 3, 5, 2, 6, 1, 7):
        remote(
            slices.at[y], slices.at[y], ag_s.at[d - 1], ag_r.at[y], device(x, lax.rem(y + d, NY), z, core)
        ).start()

    sums = [jnp.zeros((ROWS, LANES), F32) for _ in range(GROUPS)]
    for d in (0, 1, 7, 2, 6, 3, 5, 4):
        yy = lax.rem(y + d, NY)
        if d:
            arrived(slices.at[yy], ag_r.at[yy])
        for t in range(TILES):
            tile = slice(t * LANES, (t + 1) * LANES)
            rows = slices[yy, :, tile].astype(F32)
            size = rows * rows
            gain = square[yy, :, tile]
            for g in range(GROUPS):
                sums[g] = sums[g] + size * gain[g : g + 1, :]
    for d in range(1, 8):
        p = lax.rem(piece + d, 8)
        arrived(meta.at[p], mr.at[p])
    about_lanes = meta[0]
    for p in range(1, 8):
        about_lanes = about_lanes + meta[p]
    label_lane = about_lanes[0:1, :]
    half_lane = about_lanes[1:2, :]
    penalty = jnp.zeros((ROWS, LANES), F32)
    for g in range(GROUPS):
        power = jnp.sum(sums[g], axis=1, keepdims=True)
        penalty = penalty + jnp.where(label_lane == g, 0.5 * power, 0.0)

    keep_copy.wait()
    for d in range(1, 8):
        p = lax.rem(piece + d, 8)
        arrived(prep.at[p], pr.at[p])
    cross = jnp.zeros((ROWS, LANES), F32)
    for b in range(NY):
        rows = prep[:, :, b * BLOCK : (b + 1) * BLOCK].reshape(LANES, BLOCK)
        cross = cross + lax.dot_general(slices[b], rows, (((1,), (1,)), ((), ())), preferred_element_type=F32)
    value = cross - penalty
    logit[...] = jnp.where(half_lane == 0, value[0:8, :], value[8:16, :])
    for d in range(1, 8):
        remote(logit, logit_in.at[piece], ls.at[d - 1], lr.at[piece], along_x(d)).start()
    logit_in[piece] = logit[...]
    for d in range(1, 8):
        p = lax.rem(piece + d, 8)
        arrived(logit_in.at[p], lr.at[p])
    logits = logit_in[0]
    for p in range(1, 8):
        logits = logits + logit_in[p]
    highest = jnp.max(logits, axis=0, keepdims=True)
    log_total = highest + jnp.log(jnp.sum(jnp.exp(logits - highest), axis=0, keepdims=True))
    weights = jnp.exp(logits - log_total)
    both = [jnp.where(half_lane == h, weights, 0.0) for h in range(2)]
    weight[...] = jnp.concatenate(both, axis=0).astype(BF16)
    shares = weight[...]

    def weighted(yy):
        span = pl.ds(pl.multiple_of(yy * BLOCK, LANES), BLOCK)
        return jnp.dot(shares, prep[:, :, span].reshape(LANES, BLOCK), preferred_element_type=F32)

    for d in (4, 3, 5, 2, 6, 1, 7):
        yy = lax.rem(y + d, NY)
        y_out[d - 1] = weighted(yy).astype(BF16)
        remote(
            y_out.at[d - 1], y_in.at[d - 1], ys.at[d - 1], yr.at[d - 1], device(x, yy, z, core)
        ).start()
    block = weighted(y)
    lane_sets = [log_total[:, p * MINE : (p + 1) * MINE] for p in range(8)]
    chosen = lane_sets[0]
    for p in range(1, 8):
        chosen = jnp.where(piece == p, lane_sets[p], chosen)
    log_out[...] = chosen
    for d in (0, 6, 1, 5, 2, 4, 3):
        arrived(y_in.at[d], yr.at[d])
        block = block + y_in[d].astype(F32)
    own[...] = block
    z_out[...] = block.astype(BF16)

    t_copies = [
        remote(z_out, total_in.at[z], ts.at[d], tr.at[z], device(x, y, 2 * lax.rem(zh + d, 4) + core, 1))
        for d in range(4)
    ]
    for d in (2, 1, 3):
        t_copies[d].start()
    stays = (core == zl) & (core == 1)

    @pl.when(~stays)
    def _():
        t_copies[0].start()

    total_copy = remote(total, total, core_send.at[1], core_recv.at[1], partner)

    @pl.when(core == 1)
    def _():
        @pl.when(stays)
        def _():
            total[...] = own[...]

        @pl.when(~stays)
        def _():
            arrived(total_in.at[z], tr.at[z])
            total[...] = total_in[z].astype(F32)

        value = total[...]
        for d in (1, 7, 2, 6, 3, 5, 4):
            s = lax.rem(z + d, NZ)
            arrived(total_in.at[s], tr.at[s])
            value = value + total_in[s].astype(F32)
        total[...] = value
        total_copy.start()

    @pl.when(core != 1)
    def _():
        total_copy.wait_recv()

    left(part.at[far], core_send.at[0])
    for d in range(7):
        left(meta.at[piece], ms.at[d])
        left(slices.at[y], ag_s.at[d])
        left(logit, ls.at[d])
        left(y_out.at[d], ys.at[d])
        left(own_half, zs.at[d + 1])
        left(staged.at[d], ps.at[d + 1])
    for d in range(1, 4):
        left(z_out, ts.at[d])

    @pl.when(core != zl)
    def _():
        left(own_half, zs.at[0])

    @pl.when(~stays)
    def _():
        left(z_out, ts.at[0])

    @pl.when(core == 1)
    def _():
        left(total, core_send.at[1])


def insert_kernel(orient, total, log_in, log_out, volume_out):
    tents = tents_of(orient, lax.axis_index("slab"), lax.axis_index("work"))
    log_out[...] = log_in[...]
    for t in range(TILES):
        tile = slice(t * LANES, (t + 1) * LANES)
        rows = total[:, tile]
        found = [jnp.zeros((PLANES, LANES), F32) for _ in range(2)]
        for o in range(ORIENTS):
            near = tents(t, o)
            for h in range(2):
                found[h] = found[h] + near * rows[h * ORIENTS + o : h * ORIENTS + o + 1, :]
        for h in range(2):
            volume_out[h, :, tile] = found[h]


def body(particle_data, optics_label, half_set, shift_offset, ctf_bank, noise_power, half_maps, orient_index):
    dma = pltpu.SemaphoreType.DMA
    smem = pl.BlockSpec(memory_space=pltpu.SMEM)
    vmem = pl.BlockSpec(memory_space=pltpu.VMEM)
    anywhere = pl.BlockSpec(memory_space=pl.ANY)
    log_total, total = pl.pallas_call(
        kernel,
        out_shape=(
            jax.ShapeDtypeStruct((1, MINE), F32),
            jax.ShapeDtypeStruct((ROWS, BLOCK), F32),
        ),
        in_specs=[anywhere] * 8,
        out_specs=(vmem, vmem),
        scratch_shapes=[
            pltpu.SMEM((ORIENTS,), jnp.int32),
            pltpu.SMEM((MINE,), jnp.int32),
            pltpu.SMEM((MINE,), jnp.int32),
            pltpu.SMEM((2, MINE), jnp.int32),
            pltpu.VMEM((2, PLANES, BLOCK), BF16),
            pltpu.VMEM((MINE, 2 * PIX), BF16),
            pltpu.VMEM((GROUPS, PIX), F32),
            pltpu.VMEM((1, PIX), F32),
            pltpu.VMEM((2, ORIENTS, BLOCK), F32),
            pltpu.VMEM((ORIENTS, BLOCK), F32),
            pltpu.VMEM((ORIENTS, BLOCK), F32),
            pltpu.VMEM((8, ORIENTS, BLOCK), F32),
            pltpu.VMEM((NY, ROWS, BLOCK), BF16),
            pltpu.VMEM((8, ORIENTS, LANES), jnp.int32),
            pltpu.VMEM((NY, GROUPS, BLOCK), F32),
            pltpu.VMEM((PIX // ORDER, 2, MINE, LANES), F32),
            pltpu.VMEM((2, 2, MINE, LANES), F32),
            pltpu.VMEM((8, MINE, CHUNK), BF16),
            pltpu.VMEM((8, MINE, CHUNK), BF16),
            pltpu.VMEM((ORIENTS, LANES), F32),
            pltpu.VMEM((8, ORIENTS, LANES), F32),
            pltpu.VMEM((ROWS, LANES), BF16),
            pltpu.VMEM((ROWS, BLOCK), F32),
            pltpu.VMEM((7, ROWS, BLOCK), BF16),
            pltpu.VMEM((7, ROWS, BLOCK), BF16),
            pltpu.VMEM((ROWS, BLOCK), BF16),
            pltpu.VMEM((NZ, ROWS, BLOCK), BF16),
            dma((8,)),
            dma((2,)),
            dma((2,)),
            dma((7,)),
            dma((8,)),
            dma((8,)),
            dma((8,)),
            dma((8,)),
            dma((8,)),
            dma((7,)),
            dma((8,)),
            dma((7,)),
            dma((8,)),
            dma((7,)),
            dma((7,)),
            dma((4,)),
            dma((8,)),
        ],
        compiler_params=pltpu.CompilerParams(
            collective_id=0, has_side_effects=True, vmem_limit_bytes=64 * 1024 * 1024
        ),
        name="score_and_insert",
    )(
        orient_index, optics_label, half_set, shift_offset.T, half_maps, particle_data, ctf_bank,
        noise_power.reshape(1, PIX),
    )
    log_total, volume = pl.pallas_call(
        insert_kernel,
        out_shape=(
            jax.ShapeDtypeStruct((1, MINE), F32),
            jax.ShapeDtypeStruct((2, PLANES, BLOCK), F32),
        ),
        in_specs=[smem, vmem, vmem],
        out_specs=(vmem, vmem),
        name="insert",
    )(orient_index, total, log_total)
    return log_total.reshape(MINE), volume


def solution(mesh):
    placed = (
        P(("slab", "work"), None),
        P(("slab", "work")),
        P(("slab", "work")),
        P(("slab", "work"), None),
        P(),
        P(),
        P(None, "slab", "work"),
        P(),
    )
    return jax.shard_map(
        body,
        mesh=mesh,
        in_specs=placed,
        out_specs=(P(("slab", "work")), P(None, "slab", "work")),
        check_vma=False,
    )
```

```python
import math

import jax
import jax.numpy as jnp
from jax import lax
from jax.experimental import pallas as pl
from jax.experimental.pallas import tpu as pltpu
from jax.sharding import PartitionSpec as P

ORDER = 256
PIX = 20480
GRID = 4608
GROUPS = 8
ORIENTS = 8
NX, NY, NZ = 4, 8, 8
PLANES = 32
BLOCK = 640
CHUNK = NY * BLOCK
ROWS = 2 * ORIENTS
MINE = 16
LANES = 128
TILES = BLOCK // LANES
MESH = pl.DeviceIdType.MESH
F32 = jnp.float32
BF16 = jnp.bfloat16


def device(x, y, z, core):
    return {
        "slab": lax.div(z, 2) * 2 + core,
        "work": (x * 2 + lax.rem(z, 2)) * NY + y,
    }


def turn_of(steps):
    k = lax.bitwise_and(steps, 255)
    quadrant = lax.shift_right_logical(k + 32, 6)
    r = (k - 64 * quadrant).astype(F32) * F32(2.0 * math.pi / ORDER)
    r2 = r * r
    s = r * (1.0 + r2 * (-1.0 / 6 + r2 * (1.0 / 120 + r2 * (-1.0 / 5040 + r2 * (1.0 / 362880)))))
    c = 1.0 + r2 * (-0.5 + r2 * (1.0 / 24 + r2 * (-1.0 / 720 + r2 * (1.0 / 40320 - r2 * (1.0 / 3628800)))))
    odd = lax.bitwise_and(quadrant, 1) == 1
    low = jnp.where(odd, s, c)
    high = jnp.where(odd, c, s)
    turned = lax.bitwise_and(quadrant, 3)
    cosine = jnp.where((turned == 1) | (turned == 2), -low, low)
    sine = jnp.where(turned >= 2, -high, high)
    return cosine, -sine


def tents_of(orient, slab, work):
    row = lax.broadcasted_iota(jnp.int32, (ORIENTS, LANES), 0)
    index = jnp.zeros((ORIENTS, LANES), jnp.int32)
    for o in range(ORIENTS):
        index = jnp.where(row == o, orient[o], index)
    sines = jnp.sin(math.pi * (index.astype(F32) + 0.5) / GRID - 0.5 * math.pi)
    plane = (slab * PLANES + lax.broadcasted_iota(jnp.int32, (PLANES, LANES), 0)).astype(F32)
    lane = lax.broadcasted_iota(jnp.int32, (1, LANES), 1)

    def tents(t, o):
        coord_v = (lane - LANES + LANES * lax.rem(work + t, 2)).astype(F32)
        depth = ORDER // 2 + sines[o : o + 1, :] * coord_v
        return jnp.maximum(0.0, 1.0 - jnp.abs(plane - depth))

    return tents


def kernel(
    orient_in, label_in, half_in, shift_in, maps_in, data_in, ctf_in, noise_in,
    log_out, total,
    orient, label, half, shift, maps, data, ctf, noise,
    part, swap, own_half, z_in, slices, meta, square, turn_u, turn_v, staged, prep,
    logit, logit_in, weight, own, y_out, y_in, z_out, total_in,
    local_sem, core_send, core_recv, ms, mr, ps, pr, zs, zr, ag_s, ag_r, ls, lr, ys, yr, ts, tr,
):
    slab = lax.axis_index("slab")
    work = lax.axis_index("work")
    core = lax.rem(slab, 2)
    zh = lax.div(slab, 2)
    x = lax.div(work, 2 * NY)
    zl = lax.rem(lax.div(work, NY), 2)
    y = lax.rem(work, NY)
    z = 2 * zh + zl
    far = 1 - core
    partner = device(x, y, z, far)
    piece = 2 * x + core

    def remote(src, dst, send, recv, target):
        return pltpu.make_async_remote_copy(
            src_ref=src, dst_ref=dst, send_sem=send, recv_sem=recv, device_id=target, device_id_type=MESH
        )

    def arrived(dst, recv):
        remote(dst, dst, recv, recv, partner).wait_recv()

    def left(src, send):
        remote(src, src, send, send, partner).wait_send()

    def along_x(d):
        q = lax.rem(piece + d, 2 * NX)
        return device(lax.div(q, 2), y, z, lax.rem(q, 2))

    barrier = pltpu.get_barrier_semaphore()
    friends = [along_x(d) for d in range(1, 2 * NX)]
    friends += [device(x, y, lax.rem(z + d, NZ), k) for d in range(1, NZ) for k in range(2)]
    friends += [device(x, lax.rem(y + d, NY), z, core) for d in range(1, NY)]
    for friend in friends:
        pl.semaphore_signal(barrier, inc=1, device_id=friend, device_id_type=MESH)

    pairs = [
        (orient_in, orient), (maps_in, maps), (label_in, label), (half_in, half), (shift_in, shift),
        (data_in, data), (ctf_in, ctf), (noise_in, noise),
    ]
    local = [pltpu.make_async_copy(src, dst, local_sem.at[i]) for i, (src, dst) in enumerate(pairs)]
    for copy in local:
        copy.start()

    local[0].wait()
    local[1].wait()
    tents = tents_of(orient, slab, work)
    for t in range(TILES):
        tile = slice(t * LANES, (t + 1) * LANES)
        values = [maps[h, :, tile].astype(F32) for h in range(2)]
        found = [[], []]
        for o in range(ORIENTS):
            near = tents(t, o)
            for h in range(2):
                found[h].append(jnp.sum(near * values[h], axis=0, keepdims=True))
        for h in range(2):
            part[h, :, tile] = jnp.concatenate(found[h], axis=0)

    for copy in local[2:5]:
        copy.wait()
    row8 = lax.broadcasted_iota(jnp.int32, (ORIENTS, LANES), 0)
    lane8 = lax.broadcasted_iota(jnp.int32, (ORIENTS, LANES), 1)
    row16 = lax.broadcasted_iota(jnp.int32, (MINE, LANES), 0)
    lane16 = lax.broadcasted_iota(jnp.int32, (MINE, LANES), 1)
    about = [jnp.zeros((MINE, LANES), jnp.int32) for _ in range(3)]
    across = jnp.zeros((ORIENTS, LANES), jnp.int32)
    for i in range(MINE):
        here = row16 == i
        about[0] = jnp.where(here, label[i], about[0])
        about[1] = jnp.where(here, shift[0, i], about[1])
        about[2] = jnp.where(here, shift[1, i], about[2])
        there = lane8 == piece * MINE + i
        across = jnp.where(there, jnp.where(row8 == 0, label[i], half[i]), across)
    meta[piece] = across
    meta_copies = [remote(meta.at[piece], meta.at[piece], ms.at[d - 1], mr.at[piece], along_x(d)) for d in range(1, 8)]

    for v in range(2):
        cosine, sine = turn_of((lane16 + (v - 1) * LANES) * about[2])
        turn_v[v, 0] = cosine
        turn_v[v, 1] = sine
    cosine, sine = turn_of(lane16 * about[1])
    for u in range(PIX // ORDER):
        turn_u[u, 0] = jnp.broadcast_to(cosine[:, u : u + 1], (MINE, LANES))
        turn_u[u, 1] = jnp.broadcast_to(sine[:, u : u + 1], (MINE, LANES))
    bits = [lax.bitwise_and(about[0], 1 << j) != 0 for j in range(3)]

    for copy in local[5:]:
        copy.wait()

    def prepare(q, k, keep):
        def step(pair, carry):
            span = pl.ds(pl.multiple_of(q * (2 * CHUNK) + k * CHUNK + pair * (2 * BLOCK), LANES), 2 * BLOCK)
            imag_span = pl.ds(pl.multiple_of(PIX + q * (2 * CHUNK) + k * CHUNK + pair * (2 * BLOCK), LANES), 2 * BLOCK)
            filters = ctf[:, span]
            variance = noise[:, span]
            scaled = filters / variance
            real_rows = data[:, span]
            imag_rows = data[:, imag_span]
            if keep:
                squared = filters * filters / variance
            for t in range(2 * TILES):
                tile = slice(t * LANES, (t + 1) * LANES)
                if keep:
                    square[pair * 2 + t // TILES, :, (t % TILES) * LANES : (t % TILES + 1) * LANES] = squared[:, tile]
                wide = [jnp.broadcast_to(scaled[g : g + 1, tile], (MINE, LANES)) for g in range(GROUPS)]
                wide = [jnp.where(bits[0], wide[2 * j + 1], wide[2 * j]) for j in range(4)]
                wide = [jnp.where(bits[1], wide[2 * j + 1], wide[2 * j]) for j in range(2)]
                factor = jnp.where(bits[2], wide[1], wide[0])
                u = (2 * q + k) * (CHUNK // ORDER) + pair * 5 + t // 2
                cos_u, sin_u, cos_v, sin_v = turn_u[u, 0], turn_u[u, 1], turn_v[t % 2, 0], turn_v[t % 2, 1]
                cos_q = cos_u * cos_v - sin_u * sin_v
                sin_q = sin_u * cos_v + cos_u * sin_v
                real = real_rows[:, tile].astype(F32)
                imag = imag_rows[:, tile].astype(F32)
                place = pl.ds(pl.multiple_of(pair * (2 * BLOCK) + t * LANES, LANES), LANES)
                staged[2 * q + k, :, place] = ((real * cos_q - imag * sin_q) * factor).astype(BF16)
                staged[2 * (q + 2) + k, :, place] = ((real * sin_q + imag * cos_q) * factor).astype(BF16)
            return carry

        lax.fori_loop(0, NY // 2, step, 0)

    parity = lax.rem(x, 2)

    def part_copy(e, k):
        xx = lax.rem(x + e, NX)
        slot = 2 * e + (0 if k is core else 1)
        return remote(staged.at[2 * xx + k], prep.at[piece], ps.at[slot], pr.at[piece], device(xx, y, z, k))

    prepare(lax.rem(parity + 1, 2), far, False)
    prepare(parity, far, False)
    pl.semaphore_wait(barrier, len(friends))

    swap_copy = remote(part.at[far], swap, core_send.at[0], core_recv.at[0], partner)
    swap_copy.start()

    for e in (1, 2, 3):
        part_copy(e, far).start()
    part_copy(0, far).start()

    prepare(lax.rem(parity + 1, 2), core, False)
    prepare(parity, core, True)
    for e in (1, 2, 3):
        part_copy(e, core).start()
    keep_copy = pltpu.make_async_copy(staged.at[piece], prep.at[piece], ps.at[0])
    keep_copy.start()
    for copy in meta_copies:
        copy.start()

    swap_copy.wait_recv()
    own_half[...] = part[core] + swap[...]
    z_copies = [
        remote(own_half, z_in.at[slab], zs.at[d], zr.at[slab], device(x, y, lax.rem(z + d, NZ), zl))
        for d in range(NZ)
    ]
    for d in (4, 3, 5, 2, 6, 1, 7):
        z_copies[d].start()

    @pl.when(core == zl)
    def _():
        z_in[slab] = own_half[...]

    @pl.when(core != zl)
    def _():
        z_copies[0].start()

    for d in range(1, 8):
        s = lax.rem(slab + d, 8)
        arrived(z_in.at[s], zr.at[s])

    @pl.when(core != zl)
    def _():
        arrived(z_in.at[slab], zr.at[slab])

    halves = [z_in[h] + z_in[2 + h] + z_in[4 + h] + z_in[6 + h] for h in range(2)]
    slices[y] = jnp.concatenate(halves, axis=0).astype(BF16)

    for d in (4, 3, 5, 2, 6, 1, 7):
        remote(
            slices.at[y], slices.at[y], ag_s.at[d - 1], ag_r.at[y], device(x, lax.rem(y + d, NY), z, core)
        ).start()

    sums = [jnp.zeros((ROWS, LANES), F32) for _ in range(GROUPS)]
    for d in (0, 1, 7, 2, 6, 3, 5, 4):
        yy = lax.rem(y + d, NY)
        if d:
            arrived(slices.at[yy], ag_r.at[yy])
        for t in range(TILES):
            tile = slice(t * LANES, (t + 1) * LANES)
            rows = slices[yy, :, tile].astype(F32)
            size = rows * rows
            gain = square[yy, :, tile]
            for g in range(GROUPS):
                sums[g] = sums[g] + size * gain[g : g + 1, :]
    for d in range(1, 8):
        p = lax.rem(piece + d, 8)
        arrived(meta.at[p], mr.at[p])
    about_lanes = meta[0]
    for p in range(1, 8):
        about_lanes = about_lanes + meta[p]
    label_lane = about_lanes[0:1, :]
    half_lane = about_lanes[1:2, :]
    penalty = jnp.zeros((ROWS, LANES), F32)
    for g in range(GROUPS):
        power = jnp.sum(sums[g], axis=1, keepdims=True)
        penalty = penalty + jnp.where(label_lane == g, 0.5 * power, 0.0)

    keep_copy.wait()
    for d in range(1, 8):
        p = lax.rem(piece + d, 8)
        arrived(prep.at[p], pr.at[p])
    cross = jnp.zeros((ROWS, LANES), F32)
    for b in range(NY):
        rows = prep[:, :, b * BLOCK : (b + 1) * BLOCK].reshape(LANES, BLOCK)
        cross = cross + lax.dot_general(slices[b], rows, (((1,), (1,)), ((), ())), preferred_element_type=F32)
    value = cross - penalty
    logit[...] = jnp.where(half_lane == 0, value[0:8, :], value[8:16, :])
    for d in (4, 5, 3, 2, 6, 7, 1):
        remote(logit, logit_in.at[piece], ls.at[d - 1], lr.at[piece], along_x(d)).start()
    logit_in[piece] = logit[...]
    for d in range(1, 8):
        p = lax.rem(piece + d, 8)
        arrived(logit_in.at[p], lr.at[p])
    logits = logit_in[0]
    for p in range(1, 8):
        logits = logits + logit_in[p]
    highest = jnp.max(logits, axis=0, keepdims=True)
    log_total = highest + jnp.log(jnp.sum(jnp.exp(logits - highest), axis=0, keepdims=True))
    weights = jnp.exp(logits - log_total)
    both = [jnp.where(half_lane == h, weights, 0.0) for h in range(2)]
    weight[...] = jnp.concatenate(both, axis=0).astype(BF16)
    shares = weight[...]

    def weighted(yy):
        span = pl.ds(pl.multiple_of(yy * BLOCK, LANES), BLOCK)
        return jnp.dot(shares, prep[:, :, span].reshape(LANES, BLOCK), preferred_element_type=F32)

    for d in (4, 3, 5, 2, 6, 1, 7):
        yy = lax.rem(y + d, NY)
        y_out[d - 1] = weighted(yy).astype(BF16)
        remote(
            y_out.at[d - 1], y_in.at[d - 1], ys.at[d - 1], yr.at[d - 1], device(x, yy, z, core)
        ).start()
    block = weighted(y)
    lane_sets = [log_total[:, p * MINE : (p + 1) * MINE] for p in range(8)]
    chosen = lane_sets[0]
    for p in range(1, 8):
        chosen = jnp.where(piece == p, lane_sets[p], chosen)
    log_out[...] = chosen
    for d in (0, 6, 1, 5, 2, 4, 3):
        arrived(y_in.at[d], yr.at[d])
        block = block + y_in[d].astype(F32)
    own[...] = block
    z_out[...] = block.astype(BF16)

    t_copies = [
        remote(z_out, total_in.at[z], ts.at[d], tr.at[z], device(x, y, 2 * lax.rem(zh + d, 4) + core, 1))
        for d in range(4)
    ]
    for d in (2, 1, 3):
        t_copies[d].start()
    stays = (core == zl) & (core == 1)

    @pl.when(~stays)
    def _():
        t_copies[0].start()

    total_copy = remote(total, total, core_send.at[1], core_recv.at[1], partner)

    @pl.when(core == 1)
    def _():
        @pl.when(stays)
        def _():
            total[...] = own[...]

        @pl.when(~stays)
        def _():
            arrived(total_in.at[z], tr.at[z])
            total[...] = total_in[z].astype(F32)

        value = total[...]
        for d in (1, 7, 2, 6, 3, 5, 4):
            s = lax.rem(z + d, NZ)
            arrived(total_in.at[s], tr.at[s])
            value = value + total_in[s].astype(F32)
        total[...] = value
        total_copy.start()

    @pl.when(core != 1)
    def _():
        total_copy.wait_recv()

    left(part.at[far], core_send.at[0])
    for d in range(7):
        left(meta.at[piece], ms.at[d])
        left(slices.at[y], ag_s.at[d])
        left(logit, ls.at[d])
        left(y_out.at[d], ys.at[d])
        left(own_half, zs.at[d + 1])
        left(staged.at[d], ps.at[d + 1])
    for d in range(1, 4):
        left(z_out, ts.at[d])

    @pl.when(core != zl)
    def _():
        left(own_half, zs.at[0])

    @pl.when(~stays)
    def _():
        left(z_out, ts.at[0])

    @pl.when(core == 1)
    def _():
        left(total, core_send.at[1])


def insert_kernel(orient, total, log_in, log_out, volume_out):
    tents = tents_of(orient, lax.axis_index("slab"), lax.axis_index("work"))
    log_out[...] = log_in[...]
    for t in range(TILES):
        tile = slice(t * LANES, (t + 1) * LANES)
        rows = total[:, tile]
        found = [jnp.zeros((PLANES, LANES), F32) for _ in range(2)]
        for o in range(ORIENTS):
            near = tents(t, o)
            for h in range(2):
                found[h] = found[h] + near * rows[h * ORIENTS + o : h * ORIENTS + o + 1, :]
        for h in range(2):
            volume_out[h, :, tile] = found[h]


def body(particle_data, optics_label, half_set, shift_offset, ctf_bank, noise_power, half_maps, orient_index):
    dma = pltpu.SemaphoreType.DMA
    smem = pl.BlockSpec(memory_space=pltpu.SMEM)
    vmem = pl.BlockSpec(memory_space=pltpu.VMEM)
    anywhere = pl.BlockSpec(memory_space=pl.ANY)
    log_total, total = pl.pallas_call(
        kernel,
        out_shape=(
            jax.ShapeDtypeStruct((1, MINE), F32),
            jax.ShapeDtypeStruct((ROWS, BLOCK), F32),
        ),
        in_specs=[anywhere] * 8,
        out_specs=(vmem, vmem),
        scratch_shapes=[
            pltpu.SMEM((ORIENTS,), jnp.int32),
            pltpu.SMEM((MINE,), jnp.int32),
            pltpu.SMEM((MINE,), jnp.int32),
            pltpu.SMEM((2, MINE), jnp.int32),
            pltpu.VMEM((2, PLANES, BLOCK), BF16),
            pltpu.VMEM((MINE, 2 * PIX), BF16),
            pltpu.VMEM((GROUPS, PIX), F32),
            pltpu.VMEM((1, PIX), F32),
            pltpu.VMEM((2, ORIENTS, BLOCK), F32),
            pltpu.VMEM((ORIENTS, BLOCK), F32),
            pltpu.VMEM((ORIENTS, BLOCK), F32),
            pltpu.VMEM((8, ORIENTS, BLOCK), F32),
            pltpu.VMEM((NY, ROWS, BLOCK), BF16),
            pltpu.VMEM((8, ORIENTS, LANES), jnp.int32),
            pltpu.VMEM((NY, GROUPS, BLOCK), F32),
            pltpu.VMEM((PIX // ORDER, 2, MINE, LANES), F32),
            pltpu.VMEM((2, 2, MINE, LANES), F32),
            pltpu.VMEM((8, MINE, CHUNK), BF16),
            pltpu.VMEM((8, MINE, CHUNK), BF16),
            pltpu.VMEM((ORIENTS, LANES), F32),
            pltpu.VMEM((8, ORIENTS, LANES), F32),
            pltpu.VMEM((ROWS, LANES), BF16),
            pltpu.VMEM((ROWS, BLOCK), F32),
            pltpu.VMEM((7, ROWS, BLOCK), BF16),
            pltpu.VMEM((7, ROWS, BLOCK), BF16),
            pltpu.VMEM((ROWS, BLOCK), BF16),
            pltpu.VMEM((NZ, ROWS, BLOCK), BF16),
            dma((8,)),
            dma((2,)),
            dma((2,)),
            dma((7,)),
            dma((8,)),
            dma((8,)),
            dma((8,)),
            dma((8,)),
            dma((8,)),
            dma((7,)),
            dma((8,)),
            dma((7,)),
            dma((8,)),
            dma((7,)),
            dma((7,)),
            dma((4,)),
            dma((8,)),
        ],
        compiler_params=pltpu.CompilerParams(
            collective_id=0, has_side_effects=True, vmem_limit_bytes=64 * 1024 * 1024
        ),
        name="score_and_insert",
    )(
        orient_index, optics_label, half_set, shift_offset.T, half_maps, particle_data, ctf_bank,
        noise_power.reshape(1, PIX),
    )
    log_total, volume = pl.pallas_call(
        insert_kernel,
        out_shape=(
            jax.ShapeDtypeStruct((1, MINE), F32),
            jax.ShapeDtypeStruct((2, PLANES, BLOCK), F32),
        ),
        in_specs=[smem, vmem, vmem],
        out_specs=(vmem, vmem),
        name="insert",
    )(orient_index, total, log_total)
    return log_total.reshape(MINE), volume


def solution(mesh):
    placed = (
        P(("slab", "work"), None),
        P(("slab", "work")),
        P(("slab", "work")),
        P(("slab", "work"), None),
        P(),
        P(),
        P(None, "slab", "work"),
        P(),
    )
    return jax.shard_map(
        body,
        mesh=mesh,
        in_specs=placed,
        out_specs=(P(("slab", "work")), P(None, "slab", "work")),
        check_vma=False,
    )
```

```python
import math

import jax
import jax.numpy as jnp
from jax import lax
from jax.experimental import pallas as pl
from jax.experimental.pallas import tpu as pltpu
from jax.sharding import PartitionSpec as P

ORDER = 256
PIX = 20480
GRID = 4608
GROUPS = 8
ORIENTS = 8
NX, NY, NZ = 4, 8, 8
PLANES = 32
BLOCK = 640
CHUNK = NY * BLOCK
ROWS = 2 * ORIENTS
MINE = 16
LANES = 128
TILES = BLOCK // LANES
MESH = pl.DeviceIdType.MESH
F32 = jnp.float32
BF16 = jnp.bfloat16


def device(x, y, z, core):
    return {
        "slab": lax.div(z, 2) * 2 + core,
        "work": (x * 2 + lax.rem(z, 2)) * NY + y,
    }


def turn_of(steps):
    k = lax.bitwise_and(steps, 255)
    quadrant = lax.shift_right_logical(k + 32, 6)
    r = (k - 64 * quadrant).astype(F32) * F32(2.0 * math.pi / ORDER)
    r2 = r * r
    s = r * (1.0 + r2 * (-1.0 / 6 + r2 * (1.0 / 120 + r2 * (-1.0 / 5040 + r2 * (1.0 / 362880)))))
    c = 1.0 + r2 * (-0.5 + r2 * (1.0 / 24 + r2 * (-1.0 / 720 + r2 * (1.0 / 40320 - r2 * (1.0 / 3628800)))))
    odd = lax.bitwise_and(quadrant, 1) == 1
    low = jnp.where(odd, s, c)
    high = jnp.where(odd, c, s)
    turned = lax.bitwise_and(quadrant, 3)
    cosine = jnp.where((turned == 1) | (turned == 2), -low, low)
    sine = jnp.where(turned >= 2, -high, high)
    return cosine, -sine


def tents_of(orient, slab, work):
    row = lax.broadcasted_iota(jnp.int32, (ORIENTS, LANES), 0)
    index = jnp.zeros((ORIENTS, LANES), jnp.int32)
    for o in range(ORIENTS):
        index = jnp.where(row == o, orient[o], index)
    sines = jnp.sin(math.pi * (index.astype(F32) + 0.5) / GRID - 0.5 * math.pi)
    plane = (slab * PLANES + lax.broadcasted_iota(jnp.int32, (PLANES, LANES), 0)).astype(F32)
    lane = lax.broadcasted_iota(jnp.int32, (1, LANES), 1)

    def tents(t, o):
        coord_v = (lane - LANES + LANES * lax.rem(work + t, 2)).astype(F32)
        depth = ORDER // 2 + sines[o : o + 1, :] * coord_v
        return jnp.maximum(0.0, 1.0 - jnp.abs(plane - depth))

    return tents


def kernel(
    orient_in, label_in, half_in, shift_in, maps_in, data_in, ctf_in, noise_in,
    log_out, total,
    orient, label, half, shift, maps, data, ctf, noise,
    part, swap, own_half, z_in, slices, meta, square, turn_u, turn_v, staged, prep,
    logit, logit_in, weight, own, y_out, y_in, z_out, total_in,
    local_sem, core_send, core_recv, ms, mr, ps, pr, zs, zr, ag_s, ag_r, ls, lr, ys, yr, ts, tr,
):
    slab = lax.axis_index("slab")
    work = lax.axis_index("work")
    core = lax.rem(slab, 2)
    zh = lax.div(slab, 2)
    x = lax.div(work, 2 * NY)
    zl = lax.rem(lax.div(work, NY), 2)
    y = lax.rem(work, NY)
    z = 2 * zh + zl
    far = 1 - core
    partner = device(x, y, z, far)
    piece = 2 * x + core

    def remote(src, dst, send, recv, target):
        return pltpu.make_async_remote_copy(
            src_ref=src, dst_ref=dst, send_sem=send, recv_sem=recv, device_id=target, device_id_type=MESH
        )

    def arrived(dst, recv):
        remote(dst, dst, recv, recv, partner).wait_recv()

    def left(src, send):
        remote(src, src, send, send, partner).wait_send()

    def along_x(d):
        q = lax.rem(piece + d, 2 * NX)
        return device(lax.div(q, 2), y, z, lax.rem(q, 2))

    barrier = pltpu.get_barrier_semaphore()
    friends = [along_x(d) for d in range(1, 2 * NX)]
    friends += [device(x, y, lax.rem(z + d, NZ), k) for d in range(1, NZ) for k in range(2)]
    friends += [device(x, lax.rem(y + d, NY), z, core) for d in range(1, NY)]
    for friend in friends:
        pl.semaphore_signal(barrier, inc=1, device_id=friend, device_id_type=MESH)

    pairs = [
        (orient_in, orient), (maps_in, maps), (label_in, label), (half_in, half), (shift_in, shift),
        (data_in, data), (ctf_in, ctf), (noise_in, noise),
    ]
    local = [pltpu.make_async_copy(src, dst, local_sem.at[i]) for i, (src, dst) in enumerate(pairs)]
    for copy in local:
        copy.start()

    local[0].wait()
    local[1].wait()
    tents = tents_of(orient, slab, work)
    for t in range(TILES):
        tile = slice(t * LANES, (t + 1) * LANES)
        values = [maps[h, :, tile].astype(F32) for h in range(2)]
        found = [[], []]
        for o in range(ORIENTS):
            near = tents(t, o)
            for h in range(2):
                found[h].append(jnp.sum(near * values[h], axis=0, keepdims=True))
        for h in range(2):
            part[h, :, tile] = jnp.concatenate(found[h], axis=0)

    for copy in local[2:5]:
        copy.wait()
    row8 = lax.broadcasted_iota(jnp.int32, (ORIENTS, LANES), 0)
    lane8 = lax.broadcasted_iota(jnp.int32, (ORIENTS, LANES), 1)
    row16 = lax.broadcasted_iota(jnp.int32, (MINE, LANES), 0)
    lane16 = lax.broadcasted_iota(jnp.int32, (MINE, LANES), 1)
    about = [jnp.zeros((MINE, LANES), jnp.int32) for _ in range(3)]
    across = jnp.zeros((ORIENTS, LANES), jnp.int32)
    for i in range(MINE):
        here = row16 == i
        about[0] = jnp.where(here, label[i], about[0])
        about[1] = jnp.where(here, shift[0, i], about[1])
        about[2] = jnp.where(here, shift[1, i], about[2])
        there = lane8 == piece * MINE + i
        across = jnp.where(there, jnp.where(row8 == 0, label[i], half[i]), across)
    meta[piece] = across
    meta_copies = [remote(meta.at[piece], meta.at[piece], ms.at[d - 1], mr.at[piece], along_x(d)) for d in range(1, 8)]

    for v in range(2):
        cosine, sine = turn_of((lane16 + (v - 1) * LANES) * about[2])
        turn_v[v, 0] = cosine
        turn_v[v, 1] = sine
    cosine, sine = turn_of(lane16 * about[1])
    for u in range(PIX // ORDER):
        turn_u[u, 0] = jnp.broadcast_to(cosine[:, u : u + 1], (MINE, LANES))
        turn_u[u, 1] = jnp.broadcast_to(sine[:, u : u + 1], (MINE, LANES))
    bits = [lax.bitwise_and(about[0], 1 << j) != 0 for j in range(3)]

    for copy in local[5:]:
        copy.wait()

    def prepare(q, k, keep):
        def step(pair, carry):
            span = pl.ds(pl.multiple_of(q * (2 * CHUNK) + k * CHUNK + pair * (2 * BLOCK), LANES), 2 * BLOCK)
            imag_span = pl.ds(pl.multiple_of(PIX + q * (2 * CHUNK) + k * CHUNK + pair * (2 * BLOCK), LANES), 2 * BLOCK)
            filters = ctf[:, span]
            variance = noise[:, span]
            scaled = filters / variance
            real_rows = data[:, span]
            imag_rows = data[:, imag_span]
            if keep:
                squared = filters * filters / variance
            for t in range(2 * TILES):
                tile = slice(t * LANES, (t + 1) * LANES)
                if keep:
                    square[pair * 2 + t // TILES, :, (t % TILES) * LANES : (t % TILES + 1) * LANES] = squared[:, tile]
                wide = [jnp.broadcast_to(scaled[g : g + 1, tile], (MINE, LANES)) for g in range(GROUPS)]
                wide = [jnp.where(bits[0], wide[2 * j + 1], wide[2 * j]) for j in range(4)]
                wide = [jnp.where(bits[1], wide[2 * j + 1], wide[2 * j]) for j in range(2)]
                factor = jnp.where(bits[2], wide[1], wide[0])
                u = (2 * q + k) * (CHUNK // ORDER) + pair * 5 + t // 2
                cos_u, sin_u, cos_v, sin_v = turn_u[u, 0], turn_u[u, 1], turn_v[t % 2, 0], turn_v[t % 2, 1]
                cos_q = cos_u * cos_v - sin_u * sin_v
                sin_q = sin_u * cos_v + cos_u * sin_v
                real = real_rows[:, tile].astype(F32)
                imag = imag_rows[:, tile].astype(F32)
                place = pl.ds(pl.multiple_of(pair * (2 * BLOCK) + t * LANES, LANES), LANES)
                staged[2 * q + k, :, place] = ((real * cos_q - imag * sin_q) * factor).astype(BF16)
                staged[2 * (q + 2) + k, :, place] = ((real * sin_q + imag * cos_q) * factor).astype(BF16)
            return carry

        lax.fori_loop(0, NY // 2, step, 0)

    parity = lax.rem(x, 2)

    def part_copy(e, k):
        xx = lax.rem(x + e, NX)
        slot = 2 * e + (0 if k is core else 1)
        return remote(staged.at[2 * xx + k], prep.at[piece], ps.at[slot], pr.at[piece], device(xx, y, z, k))

    prepare(lax.rem(parity + 1, 2), far, False)
    prepare(parity, far, False)
    pl.semaphore_wait(barrier, len(friends))

    swap_copy = remote(part.at[far], swap, core_send.at[0], core_recv.at[0], partner)
    swap_copy.start()

    for e in (2, 1, 3):
        part_copy(e, far).start()
    part_copy(0, far).start()

    prepare(lax.rem(parity + 1, 2), core, False)
    prepare(parity, core, True)
    for e in (2, 1, 3):
        part_copy(e, core).start()
    keep_copy = pltpu.make_async_copy(staged.at[piece], prep.at[piece], ps.at[0])
    keep_copy.start()
    for copy in meta_copies:
        copy.start()

    swap_copy.wait_recv()
    own_half[...] = part[core] + swap[...]
    z_copies = [
        remote(own_half, z_in.at[slab], zs.at[d], zr.at[slab], device(x, y, lax.rem(z + d, NZ), zl))
        for d in range(NZ)
    ]
    for d in (4, 3, 5, 2, 6, 1, 7):
        z_copies[d].start()

    @pl.when(core == zl)
    def _():
        z_in[slab] = own_half[...]

    @pl.when(core != zl)
    def _():
        z_copies[0].start()

    for d in range(1, 8):
        s = lax.rem(slab + d, 8)
        arrived(z_in.at[s], zr.at[s])

    @pl.when(core != zl)
    def _():
        arrived(z_in.at[slab], zr.at[slab])

    halves = [z_in[h] + z_in[2 + h] + z_in[4 + h] + z_in[6 + h] for h in range(2)]
    slices[y] = jnp.concatenate(halves, axis=0).astype(BF16)

    for d in (4, 3, 5, 2, 6, 1, 7):
        remote(
            slices.at[y], slices.at[y], ag_s.at[d - 1], ag_r.at[y], device(x, lax.rem(y + d, NY), z, core)
        ).start()

    sums = [jnp.zeros((ROWS, LANES), F32) for _ in range(GROUPS)]
    for d in (0, 1, 7, 2, 6, 3, 5, 4):
        yy = lax.rem(y + d, NY)
        if d:
            arrived(slices.at[yy], ag_r.at[yy])
        for t in range(TILES):
            tile = slice(t * LANES, (t + 1) * LANES)
            rows = slices[yy, :, tile].astype(F32)
            size = rows * rows
            gain = square[yy, :, tile]
            for g in range(GROUPS):
                sums[g] = sums[g] + size * gain[g : g + 1, :]
    for d in range(1, 8):
        p = lax.rem(piece + d, 8)
        arrived(meta.at[p], mr.at[p])
    about_lanes = meta[0]
    for p in range(1, 8):
        about_lanes = about_lanes + meta[p]
    label_lane = about_lanes[0:1, :]
    half_lane = about_lanes[1:2, :]
    penalty = jnp.zeros((ROWS, LANES), F32)
    for g in range(GROUPS):
        power = jnp.sum(sums[g], axis=1, keepdims=True)
        penalty = penalty + jnp.where(label_lane == g, 0.5 * power, 0.0)

    keep_copy.wait()
    for d in range(1, 8):
        p = lax.rem(piece + d, 8)
        arrived(prep.at[p], pr.at[p])
    cross = jnp.zeros((ROWS, LANES), F32)
    for b in range(NY):
        rows = prep[:, :, b * BLOCK : (b + 1) * BLOCK].reshape(LANES, BLOCK)
        cross = cross + lax.dot_general(slices[b], rows, (((1,), (1,)), ((), ())), preferred_element_type=F32)
    value = cross - penalty
    logit[...] = jnp.where(half_lane == 0, value[0:8, :], value[8:16, :])
    for d in (4, 5, 3, 2, 6, 7, 1):
        remote(logit, logit_in.at[piece], ls.at[d - 1], lr.at[piece], along_x(d)).start()
    logit_in[piece] = logit[...]
    for d in range(1, 8):
        p = lax.rem(piece + d, 8)
        arrived(logit_in.at[p], lr.at[p])
    logits = logit_in[0]
    for p in range(1, 8):
        logits = logits + logit_in[p]
    highest = jnp.max(logits, axis=0, keepdims=True)
    log_total = highest + jnp.log(jnp.sum(jnp.exp(logits - highest), axis=0, keepdims=True))
    weights = jnp.exp(logits - log_total)
    both = [jnp.where(half_lane == h, weights, 0.0) for h in range(2)]
    weight[...] = jnp.concatenate(both, axis=0).astype(BF16)
    shares = weight[...]

    def weighted(yy):
        span = pl.ds(pl.multiple_of(yy * BLOCK, LANES), BLOCK)
        return jnp.dot(shares, prep[:, :, span].reshape(LANES, BLOCK), preferred_element_type=F32)

    for d in (4, 3, 5, 2, 6, 1, 7):
        yy = lax.rem(y + d, NY)
        y_out[d - 1] = weighted(yy).astype(BF16)
        remote(
            y_out.at[d - 1], y_in.at[d - 1], ys.at[d - 1], yr.at[d - 1], device(x, yy, z, core)
        ).start()
    block = weighted(y)
    lane_sets = [log_total[:, p * MINE : (p + 1) * MINE] for p in range(8)]
    chosen = lane_sets[0]
    for p in range(1, 8):
        chosen = jnp.where(piece == p, lane_sets[p], chosen)
    log_out[...] = chosen
    for d in (0, 6, 1, 5, 2, 4, 3):
        arrived(y_in.at[d], yr.at[d])
        block = block + y_in[d].astype(F32)
    own[...] = block
    z_out[...] = block.astype(BF16)

    t_copies = [
        remote(z_out, total_in.at[z], ts.at[d], tr.at[z], device(x, y, 2 * lax.rem(zh + d, 4) + core, 1))
        for d in range(4)
    ]
    for d in (2, 1, 3):
        t_copies[d].start()
    stays = (core == zl) & (core == 1)

    @pl.when(~stays)
    def _():
        t_copies[0].start()

    total_copy = remote(total, total, core_send.at[1], core_recv.at[1], partner)

    @pl.when(core == 1)
    def _():
        @pl.when(stays)
        def _():
            total[...] = own[...]

        @pl.when(~stays)
        def _():
            arrived(total_in.at[z], tr.at[z])
            total[...] = total_in[z].astype(F32)

        value = total[...]
        for d in (1, 7, 2, 6, 3, 5, 4):
            s = lax.rem(z + d, NZ)
            arrived(total_in.at[s], tr.at[s])
            value = value + total_in[s].astype(F32)
        total[...] = value
        total_copy.start()

    @pl.when(core != 1)
    def _():
        total_copy.wait_recv()

    left(part.at[far], core_send.at[0])
    for d in range(7):
        left(meta.at[piece], ms.at[d])
        left(slices.at[y], ag_s.at[d])
        left(logit, ls.at[d])
        left(y_out.at[d], ys.at[d])
        left(own_half, zs.at[d + 1])
        left(staged.at[d], ps.at[d + 1])
    for d in range(1, 4):
        left(z_out, ts.at[d])

    @pl.when(core != zl)
    def _():
        left(own_half, zs.at[0])

    @pl.when(~stays)
    def _():
        left(z_out, ts.at[0])

    @pl.when(core == 1)
    def _():
        left(total, core_send.at[1])


def insert_kernel(orient_in, total_in, log_in, log_out, volume_out, orient, total, volume, sem, out_sem):
    copies = [
        pltpu.make_async_copy(src, dst, sem.at[i])
        for i, (src, dst) in enumerate(((orient_in, orient), (total_in, total), (log_in, log_out)))
    ]
    for copy in copies:
        copy.start()
    copies[0].wait()
    tents = tents_of(orient, lax.axis_index("slab"), lax.axis_index("work"))
    copies[1].wait()
    out = []
    for t in range(TILES):
        tile = slice(t * LANES, (t + 1) * LANES)
        rows = total[:, tile]
        found = [jnp.zeros((PLANES, LANES), F32) for _ in range(2)]
        for o in range(ORIENTS):
            near = tents(t, o)
            for h in range(2):
                found[h] = found[h] + near * rows[h * ORIENTS + o : h * ORIENTS + o + 1, :]
        for h in range(2):
            volume[h, :, tile] = found[h]
        out.append(pltpu.make_async_copy(volume.at[:, :, tile], volume_out.at[:, :, tile], out_sem.at[t]))
        out[-1].start()
    for copy in copies[2:] + out:
        copy.wait()


def body(particle_data, optics_label, half_set, shift_offset, ctf_bank, noise_power, half_maps, orient_index):
    dma = pltpu.SemaphoreType.DMA
    vmem = pl.BlockSpec(memory_space=pltpu.VMEM)
    anywhere = pl.BlockSpec(memory_space=pl.ANY)
    log_total, total = pl.pallas_call(
        kernel,
        out_shape=(
            jax.ShapeDtypeStruct((1, MINE), F32),
            jax.ShapeDtypeStruct((ROWS, BLOCK), F32),
        ),
        in_specs=[anywhere] * 8,
        out_specs=(vmem, vmem),
        scratch_shapes=[
            pltpu.SMEM((ORIENTS,), jnp.int32),
            pltpu.SMEM((MINE,), jnp.int32),
            pltpu.SMEM((MINE,), jnp.int32),
            pltpu.SMEM((2, MINE), jnp.int32),
            pltpu.VMEM((2, PLANES, BLOCK), BF16),
            pltpu.VMEM((MINE, 2 * PIX), BF16),
            pltpu.VMEM((GROUPS, PIX), F32),
            pltpu.VMEM((1, PIX), F32),
            pltpu.VMEM((2, ORIENTS, BLOCK), F32),
            pltpu.VMEM((ORIENTS, BLOCK), F32),
            pltpu.VMEM((ORIENTS, BLOCK), F32),
            pltpu.VMEM((8, ORIENTS, BLOCK), F32),
            pltpu.VMEM((NY, ROWS, BLOCK), BF16),
            pltpu.VMEM((8, ORIENTS, LANES), jnp.int32),
            pltpu.VMEM((NY, GROUPS, BLOCK), F32),
            pltpu.VMEM((PIX // ORDER, 2, MINE, LANES), F32),
            pltpu.VMEM((2, 2, MINE, LANES), F32),
            pltpu.VMEM((8, MINE, CHUNK), BF16),
            pltpu.VMEM((8, MINE, CHUNK), BF16),
            pltpu.VMEM((ORIENTS, LANES), F32),
            pltpu.VMEM((8, ORIENTS, LANES), F32),
            pltpu.VMEM((ROWS, LANES), BF16),
            pltpu.VMEM((ROWS, BLOCK), F32),
            pltpu.VMEM((7, ROWS, BLOCK), BF16),
            pltpu.VMEM((7, ROWS, BLOCK), BF16),
            pltpu.VMEM((ROWS, BLOCK), BF16),
            pltpu.VMEM((NZ, ROWS, BLOCK), BF16),
            dma((8,)),
            dma((2,)),
            dma((2,)),
            dma((7,)),
            dma((8,)),
            dma((8,)),
            dma((8,)),
            dma((8,)),
            dma((8,)),
            dma((7,)),
            dma((8,)),
            dma((7,)),
            dma((8,)),
            dma((7,)),
            dma((7,)),
            dma((4,)),
            dma((8,)),
        ],
        compiler_params=pltpu.CompilerParams(
            collective_id=0, has_side_effects=True, vmem_limit_bytes=64 * 1024 * 1024
        ),
        name="score_and_insert",
    )(
        orient_index, optics_label, half_set, shift_offset.T, half_maps, particle_data, ctf_bank,
        noise_power.reshape(1, PIX),
    )
    log_total, volume = pl.pallas_call(
        insert_kernel,
        out_shape=(
            jax.ShapeDtypeStruct((1, MINE), F32),
            jax.ShapeDtypeStruct((2, PLANES, BLOCK), F32),
        ),
        in_specs=[anywhere] * 3,
        out_specs=(anywhere, anywhere),
        scratch_shapes=[
            pltpu.SMEM((ORIENTS,), jnp.int32),
            pltpu.VMEM((ROWS, BLOCK), F32),
            pltpu.VMEM((2, PLANES, BLOCK), F32),
            dma((3,)),
            dma((TILES,)),
        ],
        compiler_params=pltpu.CompilerParams(vmem_limit_bytes=64 * 1024 * 1024),
        name="insert",
    )(orient_index, total, log_total)
    return log_total.reshape(MINE), volume


def solution(mesh):
    placed = (
        P(("slab", "work"), None),
        P(("slab", "work")),
        P(("slab", "work")),
        P(("slab", "work"), None),
        P(),
        P(),
        P(None, "slab", "work"),
        P(),
    )
    return jax.shard_map(
        body,
        mesh=mesh,
        in_specs=placed,
        out_specs=(P(("slab", "work")), P(None, "slab", "work")),
        check_vma=False,
    )
```
